256 devices in a mesh: blk: 8 (over x, core), cond: 32 (over z, y).
Axes of the slice: x: 4, y: 4, z: 8, core: 2. Of those that a mesh axis runs over, the one named last changes fastest.
Arguments:
- adjoint_in: float32 [32, 6, 256, 8, 128], P('cond', None, 'blk'), may hold values from -6 to 6
- source: float32 [32, 6, 256, 8, 128], P('cond', None, 'blk'), may hold values from -6 to 6
- second_coef: float32 [32, 256, 8, 128], P('cond', 'blk'), may hold values from 0.05 to 0.5
- fourth_coef: float32 [32, 256, 8, 128], P('cond', 'blk'), may hold values from 0.02 to 0.08
- time_step: float32 [32, 256, 8, 128], P('cond', 'blk'), may hold values from 0.08 to 0.25
- jacobians: float32 [32, 2, 6, 6], P('cond'), may hold values from -2.5 to 2.5
- cond_weight: float32 [32], P('cond'), may hold values from 0.05 to 0.2
- wall_grad: float32 [32, 6, 256, 128], P('cond', None, 'blk'), may hold values from -6 to 6
- wall_mask: int32 [256, 128], P('blk'), may hold values 0 or 1
- face_perm: int32 [8, 2, 128, 128], P('blk'), may hold values from 0 to 1, as said below
- lengths: int32 [8], P('blk'), may hold values from 8 to 32, as said below
Outputs:
- adjoint_out: float32 [32, 6, 256, 8, 128], P('cond', None, 'blk')
- sensitivity: float32 [256, 128], P('blk')
The draws below stay inside these ranges and needn't reach their ends.
Inputs may be any that keep to these rules, and one draw needn't show every extreme that they name: face_perm[b, 0] and face_perm[b, 1] have exactly one 1 in each row and column; face_perm[b, 1] is the transpose of face_perm[b + 1, 0], blocks taken around the loop. `lengths`: at least one block has exactly 32 active cells.
All inputs are finite; a program needn't handle non-finite values. No bound on the sum of `wall_mask` on one device may be relied on, other than what follows from the above.
Results may differ from the reference program's by a relative error of at most 0.0001.
Values sent between devices are 32-bit elements; how exact they have to be, the bound alone decides.
No kernel may reach another device: no remote copies, remote signals or barrier semaphores. Data moves between devices by JAX's collectives and lax.ppermute only.
A program may use at most 64 MiB of HBM per device.

```python
import math
import jax
import jax.numpy as jnp
from jax import lax

NV = 6
COND = 32
J = 8
K = 128
IMAX = 32
ITERS = 2
BLOCKS = 8


def draw_face_perm(key, part):
    key = jax.random.fold_in(key, 11)
    block_keys = jax.random.split(key, BLOCKS)
    orders = jax.vmap(lambda block_key: jax.random.permutation(block_key, K))(block_keys)
    front_perm = (orders[:, :, None] == jnp.arange(K)[None, None, :]).astype(jnp.int32)
    back_perm = jnp.transpose(jnp.roll(front_perm, -1, axis=0), (0, 2, 1))
    return jnp.stack([front_perm, back_perm], axis=1)


def draw_lengths(key, part):
    key = jax.random.fold_in(key, 12)
    key_counts, key_peak = jax.random.split(key)
    counts = jax.random.randint(key_counts, (BLOCKS,), IMAX // 4, IMAX + 1)
    peak_block = jax.random.randint(key_peak, (), 0, BLOCKS)
    return jnp.where(jnp.arange(BLOCKS) == peak_block, IMAX, counts).astype(jnp.int32)


def touch_ends(array, key, low, top_value):
    longest = array.shape.index(max(array.shape))
    spots = []
    for shift in (0, 1):
        where = [jax.random.randint(jax.random.fold_in(key, axis), (), 0, length) for axis, length in enumerate(array.shape)]
        where[longest] = (where[longest] + shift) % array.shape[longest]
        spots.append(tuple(where))
    return array.at[spots[0]].set(low).at[spots[1]].set(top_value)


def block_scale(own_key, shape, shards, least, top_value):
    level = 1.0
    for dim, shards_of in shards:
        heights = jax.random.uniform(jax.random.fold_in(jax.random.fold_in(own_key, 6), dim), (shards_of,), jnp.float32, least / len(shards), top_value / len(shards))
        level = level * jnp.repeat(jnp.exp(heights), shape[dim] // shards_of).reshape((-1,) + (1,) * (len(shape) - 1 - dim))
    return level


def normal_values(stream_key, dims, scale, reach, cuts=(), held_as=jnp.bfloat16):
    factor_of = block_scale(stream_key, dims, cuts, -0.22, 0.18) if cuts else 1.0
    entries = jax.random.normal(stream_key, dims, jnp.float32) * scale * factor_of
    return jnp.minimum(jnp.maximum(entries, -reach), reach).astype(held_as)


def setup_inputs(seed: int = 0) -> dict:
    streams_of = jax.random.split(jax.random.key(seed), 12)
    return {
        "adjoint_in": normal_values(streams_of[0], (COND, NV, BLOCKS * IMAX, J, K), 1.0, 6.0, ((0, 32), (2, 8)), jnp.float32),
        "source": normal_values(streams_of[1], (COND, NV, BLOCKS * IMAX, J, K), 1.0, 6.0, ((0, 32), (2, 8)), jnp.float32),
        "second_coef": jnp.clip(jnp.exp(math.log(0.5) - 2.3025851 * jax.random.uniform(streams_of[2], (COND, BLOCKS * IMAX, J, K), jnp.float32) ** block_scale(streams_of[2], (COND, BLOCKS * IMAX, J, K), ((0, 32), (1, 8)), -0.2, 0.2)), 0.05, 0.5),
        "fourth_coef": jnp.clip(jnp.exp(math.log(0.08) - 1.3862944 * jax.random.uniform(streams_of[3], (COND, BLOCKS * IMAX, J, K), jnp.float32) ** block_scale(streams_of[3], (COND, BLOCKS * IMAX, J, K), ((0, 32), (1, 8)), -0.2, 0.2)), 0.02, 0.08),
        "time_step": jnp.clip(jnp.exp(math.log(0.25) - 1.1394343 * jax.random.uniform(streams_of[4], (COND, BLOCKS * IMAX, J, K), jnp.float32) ** block_scale(streams_of[4], (COND, BLOCKS * IMAX, J, K), ((0, 32), (1, 8)), -0.2, 0.2)), 0.08, 0.25),
        "jacobians": normal_values(streams_of[5], (COND, 2, NV, NV), NV ** -0.5, 2.5, ((0, 32),), jnp.float32),
        "cond_weight": jnp.clip(jnp.exp(math.log(0.2) - 1.3862944 * jax.random.uniform(streams_of[6], (COND,), jnp.float32) ** block_scale(streams_of[6], (COND,), ((0, 32),), -0.2, 0.2)), 0.05, 0.2),
        "wall_grad": normal_values(streams_of[7], (COND, NV, BLOCKS * IMAX, K), 1.0, 6.0, ((0, 32), (2, 8)), jnp.float32),
        "wall_mask": touch_ends((jax.random.randint(streams_of[8], (BLOCKS * IMAX, K), 0, 4) < 3).astype(jnp.int32), jax.random.fold_in(streams_of[8], 1), 0, 1),
        "face_perm": draw_face_perm(jax.random.fold_in(streams_of[11], 71), 0),
        "lengths": draw_lengths(jax.random.fold_in(streams_of[11], 71), 0),
    }


PRECISE = lax.Precision.HIGHEST
RK_FACTORS = (0.6, 0.6, 1.0)


def permute_span(values, perm):
    return jnp.einsum("cvijm,km->cvijk", values, perm, precision=PRECISE)


def extend_block(values, before, beyond, active_len, layers):
    new_shape = values.shape[:2] + (values.shape[2] + 2 * layers,) + values.shape[3:]
    grown = jnp.zeros(new_shape, jnp.float32)
    grown = lax.dynamic_update_slice_in_dim(grown, before, 0, 2)
    grown = lax.dynamic_update_slice_in_dim(grown, values, layers, 2)
    grown = lax.dynamic_update_slice_in_dim(grown, beyond, active_len + layers, 2)
    return grown


def adjoint_operator(extended, damp_two, damp_four, jacobians):
    length = extended.shape[2]
    damped_two = damp_two[:, None] * extended
    damped_four = damp_four[:, None] * extended
    centre = extended[:, :, 2:length - 2]
    diff_along = extended[:, :, 3:length - 1] - extended[:, :, 1:length - 3]
    second_along = damped_two[:, :, 3:length - 1] - 2.0 * damped_two[:, :, 2:length - 2] + damped_two[:, :, 1:length - 3]
    fourth_along = (damped_four[:, :, 4:] - 4.0 * damped_four[:, :, 3:length - 1] + 6.0 * damped_four[:, :, 2:length - 2]
                    - 4.0 * damped_four[:, :, 1:length - 3] + damped_four[:, :, :length - 4])
    edges = ((0, 0), (0, 0), (0, 0), (1, 1), (0, 0))
    padded_centre = jnp.pad(centre, edges)
    diff_across = padded_centre[:, :, :, 2:] - padded_centre[:, :, :, :-2]
    damped_mid = damped_two[:, :, 2:length - 2]
    damped_pad = jnp.pad(damped_mid, edges)
    second_across = damped_pad[:, :, :, 2:] - 2.0 * damped_mid + damped_pad[:, :, :, :-2]
    flux_total = (jnp.einsum("cuv,cuijk->cvijk", jacobians[:, 0], diff_along, precision=PRECISE)
                  + jnp.einsum("cuv,cuijk->cvijk", jacobians[:, 1], diff_across, precision=PRECISE))
    return -0.5 * flux_total - second_along + fourth_along - second_across


def reference(adjoint_in, source, second_coef, fourth_coef, time_step, jacobians, cond_weight, wall_grad, wall_mask, face_perm, lengths):
    blocks = lengths.shape[0]
    slot_count = adjoint_in.shape[2] // blocks

    def split(values):
        new_shape = values.shape[:2] + (blocks, slot_count) + values.shape[3:]
        return jnp.moveaxis(values.reshape(new_shape), 2, 0)

    active = (lax.iota(jnp.int32, slot_count)[None, :] < lengths[:, None]).astype(jnp.float32)
    state_mask = active[:, None, None, :, None, None]
    front_perm = face_perm[:, 0].astype(jnp.float32)
    back_perm = face_perm[:, 1].astype(jnp.float32)

    def neighbours(values, layers):
        lead_rim = values[:, :, :, :layers]
        tail_rim = jax.vmap(lambda block_field, active_len: lax.dynamic_slice_in_dim(block_field, active_len - layers, layers, 2))(values, lengths)
        before = jax.vmap(permute_span)(jnp.roll(tail_rim, 1, axis=0), front_perm)
        beyond = jax.vmap(permute_span)(jnp.roll(lead_rim, -1, axis=0), back_perm)
        return before, beyond

    adjoint = split(adjoint_in) * state_mask
    forcing = split(source)
    step_size = split(time_step[:, None])
    damping = split(jnp.stack([second_coef, fourth_coef], axis=1)) * state_mask
    before, beyond = neighbours(damping, 2)
    damping_wide = lax.map(lambda inputs: extend_block(inputs[0], inputs[1], inputs[2], inputs[3], 2), (damping, before, beyond, lengths))

    def advance(anchor, operand, factor):
        front_rims, back_rims = neighbours(operand, 2)

        def one_block(inputs):
            start_field, block_field, front_rim, back_rim, active_len, damp_block, step_block, force_block, mask_block = inputs
            extended = extend_block(block_field, front_rim, back_rim, active_len, 2)
            change = adjoint_operator(extended, damp_block[:, 0], damp_block[:, 1], jacobians) + force_block
            return (start_field - factor * step_block * change) * mask_block

        return lax.map(one_block, (anchor, operand, front_rims, back_rims, lengths, damping_wide, step_size, forcing, state_mask))

    wall_weights = split(wall_grad)
    mask_blocks = wall_mask.reshape(blocks, slot_count, -1).astype(jnp.float32)
    sensitivity = jnp.zeros(mask_blocks.shape, jnp.float32)
    for sweep_index in range(ITERS):
        current = adjoint
        for factor in RK_FACTORS:
            current = advance(adjoint, current, factor)
        adjoint = current
        wall_sum = jnp.sum(adjoint[:, :, :, :, 0, :] * wall_weights * cond_weight[None, :, None, None, None], axis=(1, 2))
        sensitivity = sensitivity + wall_sum * mask_blocks
    return jnp.moveaxis(adjoint, 0, 2).reshape(adjoint_in.shape), sensitivity.reshape(wall_mask.shape)
```

```python
import functools

import jax
import jax.numpy as jnp
from jax import lax
from jax.experimental import pallas as pl
from jax.experimental.pallas import tpu as pltpu
from jax.sharding import PartitionSpec as P

NV = 6
SLOTS = 32
J = 8
K = 128
DEEP = 6
NEAR = 4
EXT = SLOTS + 2 * DEEP
PLANES = NV * DEEP + 2 * DEEP + NV * NEAR + NEAR
FACTORS = (0.6, 0.6, 1.0)
GROUP = 4

VMEM = pl.BlockSpec(memory_space=pltpu.VMEM)
SMEM = pl.BlockSpec(memory_space=pltpu.SMEM)
HBM = pl.BlockSpec(memory_space=pl.ANY)
PARAMS = pltpu.CompilerParams(vmem_limit_bytes=40 * 1024 * 1024)


def plane_spans():
    spans, at = [], 0
    for field in range(NV):
        spans.append(("state", field, at, DEEP))
        at += DEEP
    for name in ("second", "fourth"):
        spans.append((name, None, at, DEEP))
        at += DEEP
    for field in range(NV):
        spans.append(("source", field, at, NEAR))
        at += NEAR
    spans.append(("step", None, at, NEAR))
    return spans


def pack_kernel(where, state, source, second, fourth, step, on_send, cross_send, sem):
    refs = {"state": state, "source": source, "second": second, "fourth": fourth, "step": step}
    copies = []
    for side, out in ((0, cross_send), (1, on_send)):
        tail = (where[1] == 0) if side == 1 else (where[1] == 1)
        for name, field, at, depth in plane_spans():
            ref = refs[name].at[0]
            if field is not None:
                ref = ref.at[field]
            start = jnp.where(tail, where[0] - depth, 0)
            copy = pltpu.make_async_copy(ref.at[pl.ds(start, depth)], out.at[pl.ds(at, depth)], sem)
            copy.start()
            copies.append(copy)
    for copy in copies:
        copy.wait()


def index_kernel(perm, out):
    marks = lax.broadcasted_iota(jnp.int32, (J, K), 1).astype(jnp.bfloat16)
    for side in range(2):
        one_hot = perm[0, side].astype(jnp.float32).astype(jnp.bfloat16)
        found = lax.dot_general(marks, one_hot, (((1,), (1,)), ((), ())), preferred_element_type=jnp.float32)
        out[side] = found.astype(jnp.int32)


def take_span(values, index):
    return jnp.take_along_axis(values, index, axis=1, mode="promise_in_bounds")


def section(factor, first, count, jac, anchor, state, result, source, second, fourth, step, work):
    up_work, down_work, fourth_work, mid_work = work
    row = lax.broadcasted_iota(jnp.int32, (J, K), 0)
    top, bottom = row == J - 1, row == 0

    def local_terms(g, _):
        at = [first - 2 + g * GROUP + n for n in range(GROUP)]
        p = [[state[u, e] for u in range(NV)] for e in at]
        s2 = [second[e] for e in at]
        s4 = [fourth[e] for e in at]
        side = [a + 4.0 * b for a, b in zip(s2, s4)]
        centre = [4.0 * a + 6.0 * b for a, b in zip(s2, s4)]
        for v in range(NV):
            along = [jac[0, 0, 0, v] * q[0] for q in p]
            across = [jac[0, 1, 0, v] * q[0] for q in p]
            for u in range(1, NV):
                along = [a + jac[0, 0, u, v] * q[u] for a, q in zip(along, p)]
                across = [a + jac[0, 1, u, v] * q[u] for a, q in zip(across, p)]
            for n, e in enumerate(at):
                flux = 0.5 * along[n]
                damp = side[n] * p[n][v]
                up_work[v, e] = flux + damp
                down_work[v, e] = flux - damp
                fourth_work[v, e] = s4[n] * p[n][v]
                flux = 0.5 * across[n]
                damp = s2[n] * p[n][v]
                above = jnp.where(top, 0.0, pltpu.roll(flux + damp, J - 1, 0))
                below = jnp.where(bottom, 0.0, pltpu.roll(flux - damp, 1, 0))
                mid_work[v, e] = centre[n] * p[n][v] - above + below
        return 0

    def combine(g, _):
        for n in range(GROUP):
            e = first + g * GROUP + n
            scale = factor * step[e]
            for v in range(NV):
                change = (
                    mid_work[v, e]
                    - up_work[v, e + 1]
                    + down_work[v, e - 1]
                    + fourth_work[v, e + 2]
                    + fourth_work[v, e - 2]
                    + source[v, e]
                )
                result[v, e] = anchor[v, e] - scale * change
        return 0

    lax.fori_loop(0, count // GROUP + 1, local_terms, 0)
    lax.fori_loop(0, count // GROUP, combine, 0)


def round_up(value):
    return lax.div(value + (GROUP - 1), GROUP) * GROUP


def three_sections(active_len, jac, state, one, two, three, source, second, fourth, step, work):
    fields = (source, second, fourth, step, work)
    section(FACTORS[0], DEEP - 4, round_up(active_len + 8), jac, state, state, one, *fields)
    section(FACTORS[1], DEEP - 2, round_up(active_len + 4), jac, state, one, two, *fields)
    section(FACTORS[2], DEEP, round_up(active_len), jac, state, two, three, *fields)


def first_kernel(
    where, jac, index, on_got, cross_got, state_in, source_in, second_in, fourth_in, step_in,
    after, source, second, fourth, step, on_send, cross_send,
    state, one, two, up_work, down_work, fourth_work, mid_work, sem,
):
    body = pl.ds(DEEP, SLOTS)
    copies = [pltpu.make_async_copy(state_in.at[0], state.at[:, body], sem),
              pltpu.make_async_copy(source_in.at[0], source.at[:, body], sem),
              pltpu.make_async_copy(second_in.at[0], second.at[body], sem),
              pltpu.make_async_copy(fourth_in.at[0], fourth.at[body], sem),
              pltpu.make_async_copy(step_in.at[0], step.at[body], sem)]
    for copy in copies:
        copy.start()
    for copy in copies:
        copy.wait()
    active_len, odd = where[0], where[1]
    refs = {"state": state, "source": source, "second": second, "fourth": fourth, "step": step}
    for got, before in ((on_got, odd), (cross_got, 1 - odd)):
        perm = index[1 - before]
        for name, field, at, depth in plane_spans():
            ref = refs[name] if field is None else refs[name].at[field]
            base = jnp.where(before == 1, DEEP - depth, active_len + DEEP)
            for layer in range(depth):
                ref[base + layer] = take_span(got[at + layer], perm)
    three_sections(active_len, jac, state, one, two, after, source, second, fourth, step,
                   (up_work, down_work, fourth_work, mid_work))
    for out, tail in ((on_send, 1 - odd), (cross_send, odd)):
        base = jnp.where(tail == 1, active_len, DEEP)
        for v in range(NV):
            for layer in range(DEEP):
                out[v * DEEP + layer] = after[v, base + layer]


def second_kernel(
    where, jac, weight, index, on_got, cross_got, state, source, second, fourth, step, wall_grad, wall_mask,
    adjoint_out, wall_out, state_out,
    one, two, last, up_work, down_work, fourth_work, mid_work,
):
    active_len, odd = where[0], where[1]
    state = state_out
    for got, before in ((on_got, odd), (cross_got, 1 - odd)):
        perm = index[1 - before]
        base = jnp.where(before == 1, 0, active_len + DEEP)
        for v in range(NV):
            for layer in range(DEEP):
                state[v, base + layer] = take_span(got[v * DEEP + layer], perm)
    three_sections(active_len, jac, state, one, two, last, source, second, fourth, step,
                   (up_work, down_work, fourth_work, mid_work))
    live = lax.broadcasted_iota(jnp.int32, (SLOTS, K), 0) < active_len
    body = pl.ds(DEEP, SLOTS)
    total = jnp.zeros((SLOTS, K), jnp.float32)
    for v in range(NV):
        total = total + (state[v, body, 0, :] + last[v, body, 0, :]) * wall_grad[0, v]
    total = total * weight[0] * wall_mask[...].astype(jnp.float32)
    wall_out[...] = jnp.where(live, total, 0.0)
    for i in range(SLOTS):
        for v in range(NV):
            adjoint_out[0, v, i] = jnp.where(i < active_len, last[v, DEEP + i], 0.0)


def f32(*shape):
    return jax.ShapeDtypeStruct(shape, jnp.float32)


def wide(*fields):
    return f32(*fields, EXT, J, K)


def scratch(count):
    return [pltpu.VMEM((NV, EXT, J, K), jnp.float32)] * count


def sum_over_conditions(value, pairs_of):
    for shifts in (((0, 1), (0, 2), (0, 3)), ((2, 0), (4, 0), (6, 0)), ((1, 0),)):
        parts = [lax.ppermute(value, "cond", pairs_of(*shift)) for shift in shifts]
        value = functools.reduce(jnp.add, parts, value)
    return value


def body(sizes, adjoint_in, source, second_coef, fourth_coef, time_step, jacobians, cond_weight, wall_grad, wall_mask,
         face_perm, lengths):
    blocks, z_size, y_size = sizes
    place = lax.axis_index("blk")
    where = jnp.stack([lengths[0], (place % 2).astype(jnp.int32)])
    chip = [(b, b ^ 1) for b in range(blocks)]
    cross = [(b, (b + (1 if b % 2 else -1)) % blocks) for b in range(blocks)]

    def pairs_of(z_shift, y_shift):
        return [(z * y_size + y, (z + z_shift) % z_size * y_size + (y + y_shift) % y_size)
                for z in range(z_size) for y in range(y_size)]

    def exchange(on_send, cross_send):
        cross_got = lax.ppermute(cross_send, "blk", cross)
        return lax.ppermute(on_send, "blk", chip), cross_got

    fields = [pltpu.with_memory_space_constraint(x, pltpu.HBM)
              for x in (adjoint_in, source, second_coef, fourth_coef, time_step)]
    on_send, cross_send = pl.pallas_call(
        pack_kernel, name="pack_rims", out_shape=[f32(PLANES, J, K)] * 2, in_specs=[SMEM] + [HBM] * 5, out_specs=[VMEM] * 2,
        scratch_shapes=[pltpu.SemaphoreType.DMA], compiler_params=PARAMS,
    )(where, *fields)
    index = pl.pallas_call(
        index_kernel, name="span_index", out_shape=jax.ShapeDtypeStruct((2, J, K), jnp.int32), in_specs=[VMEM], out_specs=VMEM,
        compiler_params=PARAMS,
    )(face_perm)
    on_got, cross_got = exchange(on_send, cross_send)
    after, source_wide, second_wide, fourth_wide, step_wide, on_send, cross_send = pl.pallas_call(
        first_kernel, name="first_iteration",
        out_shape=[wide(NV), wide(NV), wide(), wide(), wide(), f32(NV * DEEP, J, K), f32(NV * DEEP, J, K)],
        in_specs=[SMEM, SMEM] + [VMEM] * 3 + [HBM] * 5, out_specs=[VMEM] * 7,
        scratch_shapes=scratch(7) + [pltpu.SemaphoreType.DMA], compiler_params=PARAMS,
    )(where, jacobians, index, on_got, cross_got, *fields)
    on_got, cross_got = exchange(on_send, cross_send)
    adjoint_out, wall, _ = pl.pallas_call(
        second_kernel, name="second_iteration", out_shape=[f32(1, NV, SLOTS, J, K), f32(SLOTS, K), wide(NV)],
        in_specs=[SMEM] * 3 + [VMEM] * 10, out_specs=[VMEM] * 3, scratch_shapes=scratch(7), compiler_params=PARAMS,
        input_output_aliases={6: 2},
    )(where, jacobians, cond_weight, index, on_got, cross_got, after, source_wide, second_wide, fourth_wide, step_wide,
      wall_grad, wall_mask)
    return adjoint_out, sum_over_conditions(wall, pairs_of)


def solution(mesh):
    y_size = 4
    sizes = (mesh.shape["blk"], mesh.shape["cond"] // y_size, y_size)
    return jax.shard_map(
        functools.partial(body, sizes),
        mesh=mesh,
        in_specs=(
            P("cond", None, "blk", None, None),
            P("cond", None, "blk", None, None),
            P("cond", "blk", None, None),
            P("cond", "blk", None, None),
            P("cond", "blk", None, None),
            P("cond", None, None, None),
            P("cond"),
            P("cond", None, "blk", None),
            P("blk", None),
            P("blk", None, None, None),
            P("blk"),
        ),
        out_specs=(P("cond", None, "blk", None, None), P("blk", None)),
        check_vma=False,
    )
```

```python
import functools

import jax
import jax.numpy as jnp
from jax import lax
from jax.experimental import pallas as pl
from jax.experimental.pallas import tpu as pltpu
from jax.sharding import PartitionSpec as P

NV = 6
SLOTS = 32
J = 8
K = 128
DEEP = 6
NEAR = 4
EXT = SLOTS + 2 * DEEP
PLANES = NV * DEEP + 2 * DEEP + NV * NEAR + NEAR
FACTORS = (0.6, 0.6, 1.0)
GROUP = 8
ROWS = NV * J

VMEM = pl.BlockSpec(memory_space=pltpu.VMEM)
SMEM = pl.BlockSpec(memory_space=pltpu.SMEM)
HBM = pl.BlockSpec(memory_space=pl.ANY)
PARAMS = pltpu.CompilerParams(vmem_limit_bytes=32 * 1024 * 1024)


def odd_place():
    return lax.rem(lax.axis_index("blk"), 2) == 1


def message_spans():
    at = 0
    for name, fields, depth in (("state", NV, DEEP), ("second", 1, DEEP), ("fourth", 1, DEEP), ("source", NV, NEAR), ("step", 1, NEAR)):
        for field in range(fields):
            yield name, field if fields > 1 else None, at, depth
            at += depth


def pack_kernel(lengths, state, source, second, fourth, step, on_send, cross_send, sem):
    refs = {"state": state, "source": source, "second": second, "fourth": fourth, "step": step}
    odd = odd_place()

    def start_copies(out, out_sem, tail):
        for name, field, at, depth in message_spans():
            ref = refs[name].at[0] if field is None else refs[name].at[0, field]
            first = lengths[0] - depth if tail else 0
            pltpu.make_async_copy(ref.at[pl.ds(first, depth)], out.at[pl.ds(at, depth)], out_sem).start()

    @pl.when(odd)
    def _():
        start_copies(on_send, sem.at[0], False)

    @pl.when(jnp.logical_not(odd))
    def _():
        start_copies(cross_send, sem.at[1], False)

    @pl.when(odd)
    def _():
        start_copies(cross_send, sem.at[1], True)

    @pl.when(jnp.logical_not(odd))
    def _():
        start_copies(on_send, sem.at[0], True)

    pltpu.make_async_copy(on_send, on_send, sem.at[0]).wait()
    pltpu.make_async_copy(cross_send, cross_send, sem.at[1]).wait()


def edge_rows():
    row = lax.broadcasted_iota(jnp.int32, (J, K), 0)
    return row == J - 1, row == 0


def shift_up(values):
    return pltpu.roll(values, J - 1, 0)


def shift_down(values):
    return pltpu.roll(values, 1, 0)


def two_parts(values):
    high = values.astype(jnp.bfloat16)
    return high, (values - high.astype(jnp.float32)).astype(jnp.bfloat16)


def flux_matrix(jac):
    width = 4 * ROWS
    lane = lax.broadcasted_iota(jnp.int32, (J, width), 1)
    row = lax.broadcasted_iota(jnp.int32, (J, width), 0)
    lane = jnp.where(lane >= 2 * ROWS, lane - 2 * ROWS, lane)
    pair = lane // J
    j = lane % J
    pattern = jnp.where(pair < NV, (j == row).astype(jnp.float32), (j == row + 1).astype(jnp.float32) - (j == row - 1).astype(jnp.float32))
    blocks = []
    for v in range(NV):
        block = jnp.zeros((J, width), jnp.float32)
        for axis in range(2):
            for u in range(NV):
                block = jnp.where(pair == axis * NV + u, -0.5 * jac[0, axis, u, v], block)
        blocks.append(block * pattern)
    high, low = two_parts(jnp.concatenate(blocks, 0))
    return jnp.concatenate([high, low], 0)


def flux_terms(matrix, state, cells):
    columns = []
    for e in cells:
        along = (state[:, e + 1] - state[:, e - 1]).reshape(ROWS, K)
        here = state[:, e].reshape(ROWS, K)
        high, low = two_parts(jnp.concatenate([along, here], 0))
        columns.append(jnp.concatenate([high, low], 0))
    product = jnp.dot(matrix, jnp.concatenate(columns, 1), preferred_element_type=jnp.float32)
    product = product[:ROWS] + product[ROWS:]
    return [[product[v * J : (v + 1) * J, n * K : (n + 1) * K] for v in range(NV)] for n in range(len(cells))]


def advance(factor, matrix, runs, anchor, state, result, fields):
    source, second, fourth, step = fields
    top, bottom = edge_rows()
    flux = flux_terms(matrix, state, [first + n for first, count in runs for n in range(count)])
    for first, count in runs:
        s2 = [second[first + n] for n in range(-1, count + 1)]
        s4 = [fourth[first + n] for n in range(-2, count + 2)]
        side = [a + 4.0 * b for a, b in zip(s2, s4[1:])]
        centre = [4.0 * a + 6.0 * b for a, b in zip(s2[1:], s4[2:])][:count]
        above = [jnp.where(top, 0.0, shift_up(a)) for a in s2[1 : count + 1]]
        below = [jnp.where(bottom, 0.0, shift_down(a)) for a in s2[1 : count + 1]]
        scale = [factor * step[first + n] for n in range(count)]
        for v in range(NV):
            p = [state[v, first + n] for n in range(-2, count + 2)]
            r = [a * b for a, b in zip(side, p[1:])]
            q = [a * b for a, b in zip(s4, p)]
            for n in range(count):
                here = p[n + 2]
                change = (
                    flux[n][v]
                    + centre[n] * here
                    - (r[n] + r[n + 2])
                    + (q[n] + q[n + 4])
                    - (above[n] * shift_up(here) + below[n] * shift_down(here))
                    + source[v, first + n]
                )
                result[v, first + n] = anchor[v, first + n] - scale[n] * change
        flux = flux[count:]


def interior(active_len, matrix, states, fields):
    anchor = states[0]
    for s in range(3):
        lead = 2 * (s + 1)
        groups = lax.div(jnp.maximum(active_len - 2 * lead, 0) + (GROUP - 1), GROUP)

        def step(g, _, s=s, lead=lead):
            first = DEEP + lead + g * GROUP
            advance(FACTORS[s], matrix[...], [(first, GROUP)], anchor, states[s], states[s + 1], fields)
            return 0

        lax.fori_loop(0, groups, step, 0)


def boundary(active_len, matrix, states, fields):
    anchor = states[0]
    for s in range(3):
        lead = 2 * (s + 1)
        runs = [(lead, DEEP), (active_len + DEEP - lead, DEEP)]
        advance(FACTORS[s], matrix[...], runs, anchor, states[s], states[s + 1], fields)


def span_index(perm):
    marks = lax.broadcasted_iota(jnp.int32, (J, K), 1).astype(jnp.bfloat16)
    one_hot = perm.astype(jnp.float32).astype(jnp.bfloat16)
    found = lax.dot_general(marks, one_hot, (((1,), (1,)), ((), ())), preferred_element_type=jnp.float32)
    return found.astype(jnp.int32)


def take_span(values, index):
    return jnp.take_along_axis(values, index, axis=1, mode="promise_in_bounds")


def sides(active_len, on, cross):
    odd = odd_place()
    return ((odd, on), (jnp.logical_not(odd), cross))


def first_interior_kernel(
    lengths, jac, perm, state_in, source_in, second_in, fourth_in, step_in,
    index, matrix, state, source, second, fourth, step, one, two, three,
    sem,
):
    body = pl.ds(DEEP, SLOTS)
    copies = [
        pltpu.make_async_copy(state_in.at[0], state.at[:, body], sem.at[0]),
        pltpu.make_async_copy(second_in.at[0], second.at[body], sem.at[1]),
        pltpu.make_async_copy(fourth_in.at[0], fourth.at[body], sem.at[2]),
        pltpu.make_async_copy(source_in.at[0], source.at[:, body], sem.at[3]),
        pltpu.make_async_copy(step_in.at[0], step.at[body], sem.at[4]),
    ]
    for copy in copies:
        copy.start()
    for side in range(2):
        index[side] = span_index(perm[0, side])
    matrix[...] = flux_matrix(jac)
    for copy in copies:
        copy.wait()
    interior(lengths[0], matrix, (state, one, two, three), (source, second, fourth, step))


def first_boundary_kernel(
    lengths, index, matrix, on_got, cross_got, state_in, source_in, second_in, fourth_in, step_in, one_in, two_in, three_in,
    state, source, second, fourth, step, one, two, three, on_send, cross_send,
):
    active_len = lengths[0]
    refs = {"state": state, "source": source, "second": second, "fourth": fourth, "step": step}
    for before, got in sides(active_len, on_got, cross_got):
        perm = jnp.where(before, index[0], index[1])
        for name, field, at, depth in message_spans():
            ref = refs[name] if field is None else refs[name].at[field]
            base = jnp.where(before, DEEP - depth, active_len + DEEP)
            for layer in range(depth):
                ref[base + layer] = take_span(got[at + layer], perm)
    boundary(active_len, matrix, (state, one, two, three), (source, second, fourth, step))
    for lead, out in sides(active_len, on_send, cross_send):
        base = jnp.where(lead, DEEP, active_len)
        for v in range(NV):
            for layer in range(DEEP):
                out[v * DEEP + layer] = three[v, base + layer]


def second_interior_kernel(
    lengths, matrix, state, source, second, fourth, step, wall_grad,
    one, two, three, wall_start, wall,
):
    active_len = lengths[0]
    interior(active_len, matrix, (state, one, two, three), (source, second, fourth, step))
    body = pl.ds(DEEP, SLOTS)
    start = jnp.zeros((SLOTS, K), jnp.float32)
    more = jnp.zeros((SLOTS, K), jnp.float32)
    for v in range(NV):
        start = start + state[v, body, 0, :] * wall_grad[0, v]
        more = more + three[v, body, 0, :] * wall_grad[0, v]
    slot = lax.broadcasted_iota(jnp.int32, (SLOTS, K), 0)
    wall_start[...] = start
    wall[...] = jnp.where((slot >= DEEP) & (slot < active_len - DEEP), start + more, 0.0)


def second_boundary_kernel(
    lengths, weight, index, matrix, on_got, cross_got, source, second, fourth, step, wall_grad, wall_mask, wall_start, wall_in,
    state_in, one_in, two_in, three_in,
    state, one, two, three, wall,
    rows,
):
    active_len = lengths[0]
    for before, got in sides(active_len, on_got, cross_got):
        perm = jnp.where(before, index[0], index[1])
        base = jnp.where(before, 0, active_len + DEEP)
        for v in range(NV):
            for layer in range(DEEP):
                state[v, base + layer] = take_span(got[v * DEEP + layer], perm)
    boundary(active_len, matrix, (state, one, two, three), (source, second, fourth, step))
    rows[...] = wall_in[...]
    for base in (0, active_len - DEEP):
        for layer in range(DEEP):
            slot = pl.ds(base + layer, 1)
            total = wall_start[slot]
            for v in range(NV):
                total = total + three[v, base + layer + DEEP, pl.ds(0, 1), :] * wall_grad[0, v, slot]
            rows[slot] = total
    wall[...] = rows[...] * weight[0] * wall_mask[...].astype(jnp.float32)


def f32(*shape):
    return jax.ShapeDtypeStruct(shape, jnp.float32)


def call(kernel, name, outs, ins, out_specs=None, scratch=(), aliases=None):
    return pl.pallas_call(
        kernel, name=name, out_shape=outs, in_specs=ins, out_specs=out_specs or [VMEM] * len(outs),
        scratch_shapes=list(scratch), input_output_aliases=aliases or {}, compiler_params=PARAMS,
    )


def sum_over_conditions(value, z_size, y_size):
    pairs = [(z * y_size + y, (z ^ 1) * y_size + y) for z in range(z_size) for y in range(y_size)]
    groups = [[z * y_size + y for z in range(half, z_size, 2) for y in range(y_size)] for half in range(2)]
    value = value + lax.ppermute(value, "cond", pairs)
    copies = jnp.broadcast_to(value[None], (len(groups[0]),) + value.shape)
    return lax.all_to_all(copies, "cond", 0, 0, tiled=True, axis_index_groups=groups).sum(0)


def body(blocks, z_size, y_size, adjoint_in, source, second_coef, fourth_coef, time_step, jacobians, cond_weight, wall_grad,
         wall_mask, face_perm, lengths):
    chip = [(b, b ^ 1) for b in range(blocks)]
    cross = [(b, (b + (1 if b % 2 else -1)) % blocks) for b in range(blocks)]

    def exchange(on_send, cross_send):
        cross_got = lax.ppermute(cross_send, "blk", cross)
        return lax.ppermute(on_send, "blk", chip), cross_got

    planes, plane = f32(NV, EXT, J, K), f32(EXT, J, K)
    inputs = [pltpu.with_memory_space_constraint(x, pltpu.HBM) for x in (adjoint_in, source, second_coef, fourth_coef, time_step)]
    on_send, cross_send = call(
        pack_kernel, "pack_rims", [f32(PLANES, J, K)] * 2, [SMEM] + [HBM] * 5, scratch=[pltpu.SemaphoreType.DMA((2,))],
    )(lengths, *inputs)
    on_got, cross_got = exchange(on_send, cross_send)
    index, matrix, *arrays = call(
        first_interior_kernel, "first_interior",
        [jax.ShapeDtypeStruct((2, J, K), jnp.int32), jax.ShapeDtypeStruct((2 * ROWS, 4 * ROWS), jnp.bfloat16), planes, planes,
         plane, plane, plane, planes, planes, planes],
        [SMEM, SMEM, VMEM] + [HBM] * 5, scratch=[pltpu.SemaphoreType.DMA((5,))],
    )(lengths, jacobians, face_perm, *inputs)
    _, source_x, second_x, fourth_x, step_x, _, _, three, on_send, cross_send = call(
        first_boundary_kernel, "first_boundary",
        [planes, planes, plane, plane, plane, planes, planes, planes] + [f32(NV * DEEP, J, K)] * 2,
        [SMEM] + [VMEM] * 12, aliases={5 + n: n for n in range(8)},
    )(lengths, index, matrix, on_got, cross_got, *arrays)
    fields = (source_x, second_x, fourth_x, step_x)
    on_got, cross_got = exchange(on_send, cross_send)
    four, five, six, wall_start, wall = call(
        second_interior_kernel, "second_interior", [planes] * 3 + [f32(SLOTS, K)] * 2, [SMEM] + [VMEM] * 7,
    )(lengths, matrix, three, *fields, wall_grad)
    _, _, _, six, wall = call(
        second_boundary_kernel, "second_boundary", [planes] * 4 + [f32(SLOTS, K)],
        [SMEM] * 2 + [VMEM] * 16, scratch=[pltpu.VMEM((SLOTS, K), jnp.float32)], aliases={14 + n: n for n in range(4)},
    )(lengths, cond_weight, index, matrix, on_got, cross_got, *fields, wall_grad, wall_mask, wall_start, wall, three, four, five, six)
    active = lax.iota(jnp.int32, SLOTS) < lengths[0]
    adjoint = jnp.where(active[None, None, :, None, None], six[None, :, DEEP : DEEP + SLOTS], 0.0)
    return adjoint, sum_over_conditions(wall, z_size, y_size)


def solution(mesh):
    y_size = 4
    return jax.shard_map(
        functools.partial(body, mesh.shape["blk"], mesh.shape["cond"] // y_size, y_size),
        mesh=mesh,
        in_specs=(
            P("cond", None, "blk", None, None),
            P("cond", None, "blk", None, None),
            P("cond", "blk", None, None),
            P("cond", "blk", None, None),
            P("cond", "blk", None, None),
            P("cond", None, None, None),
            P("cond"),
            P("cond", None, "blk", None),
            P("blk", None),
            P("blk", None, None, None),
            P("blk"),
        ),
        out_specs=(P("cond", None, "blk", None, None), P("blk", None)),
        check_vma=False,
    )
```

```python
import functools

import jax
import jax.numpy as jnp
from jax import lax
from jax.experimental import pallas as pl
from jax.experimental.pallas import tpu as pltpu
from jax.sharding import PartitionSpec as P

NV = 6
SLOTS = 32
J = 8
K = 128
DEEP = 6
NEAR = 4
EXT = SLOTS + 2 * DEEP
PLANES = NV * DEEP + 2 * DEEP + NV * NEAR + NEAR
FACTORS = (0.6, 0.6, 1.0)
GROUP = 8
ROWS = NV * J

VMEM = pl.BlockSpec(memory_space=pltpu.VMEM)
SMEM = pl.BlockSpec(memory_space=pltpu.SMEM)
HBM = pl.BlockSpec(memory_space=pl.ANY)
PARAMS = pltpu.CompilerParams(vmem_limit_bytes=32 * 1024 * 1024)


def odd_place():
    return lax.rem(lax.axis_index("blk"), 2) == 1


def message_spans():
    at = 0
    for name, fields, depth in (("state", NV, DEEP), ("second", 1, DEEP), ("fourth", 1, DEEP), ("source", NV, NEAR), ("step", 1, NEAR)):
        for field in range(fields):
            yield name, field if fields > 1 else None, at, depth
            at += depth


def pack_kernel(lengths, state, source, second, fourth, step, on_send, cross_send, sem):
    refs = {"state": state, "source": source, "second": second, "fourth": fourth, "step": step}
    odd = odd_place()

    def start_copies(out, out_sem, tail):
        for name, field, at, depth in message_spans():
            ref = refs[name].at[0] if field is None else refs[name].at[0, field]
            first = lengths[0] - depth if tail else 0
            pltpu.make_async_copy(ref.at[pl.ds(first, depth)], out.at[pl.ds(at, depth)], out_sem).start()

    @pl.when(odd)
    def _():
        start_copies(on_send, sem.at[0], False)

    @pl.when(jnp.logical_not(odd))
    def _():
        start_copies(cross_send, sem.at[1], False)

    @pl.when(odd)
    def _():
        start_copies(cross_send, sem.at[1], True)

    @pl.when(jnp.logical_not(odd))
    def _():
        start_copies(on_send, sem.at[0], True)

    pltpu.make_async_copy(on_send, on_send, sem.at[0]).wait()
    pltpu.make_async_copy(cross_send, cross_send, sem.at[1]).wait()


def edge_rows():
    row = lax.broadcasted_iota(jnp.int32, (J, K), 0)
    return row == J - 1, row == 0


def shift_up(values):
    return pltpu.roll(values, J - 1, 0)


def shift_down(values):
    return pltpu.roll(values, 1, 0)


def two_parts(values):
    high = values.astype(jnp.bfloat16)
    return high, (values - high.astype(jnp.float32)).astype(jnp.bfloat16)


def flux_matrix(jac):
    width = 4 * ROWS
    lane = lax.broadcasted_iota(jnp.int32, (J, width), 1)
    row = lax.broadcasted_iota(jnp.int32, (J, width), 0)
    lane = jnp.where(lane >= 2 * ROWS, lane - 2 * ROWS, lane)
    pair = lane // J
    j = lane % J
    pattern = jnp.where(pair < NV, (j == row).astype(jnp.float32), (j == row + 1).astype(jnp.float32) - (j == row - 1).astype(jnp.float32))
    blocks = []
    for v in range(NV):
        block = jnp.zeros((J, width), jnp.float32)
        for axis in range(2):
            for u in range(NV):
                block = jnp.where(pair == axis * NV + u, -0.5 * jac[0, axis, u, v], block)
        blocks.append(block * pattern)
    high, low = two_parts(jnp.concatenate(blocks, 0))
    return jnp.concatenate([high, low], 0)


def flux_terms(matrix, state, cells):
    columns = []
    for e in cells:
        along = (state[:, e + 1] - state[:, e - 1]).reshape(ROWS, K)
        here = state[:, e].reshape(ROWS, K)
        high, low = two_parts(jnp.concatenate([along, here], 0))
        columns.append(jnp.concatenate([high, low], 0))
    product = jnp.dot(matrix, jnp.concatenate(columns, 1), preferred_element_type=jnp.float32)
    product = product[:ROWS] + product[ROWS:]
    return [[product[v * J : (v + 1) * J, n * K : (n + 1) * K] for v in range(NV)] for n in range(len(cells))]


def advance(factor, matrix, runs, anchor, state, result, fields):
    source, second, fourth, step = fields
    top, bottom = edge_rows()
    flux = flux_terms(matrix, state, [first + n for first, count in runs for n in range(count)])
    for first, count in runs:
        s2 = [second[first + n] for n in range(-1, count + 1)]
        s4 = [fourth[first + n] for n in range(-2, count + 2)]
        side = [a + 4.0 * b for a, b in zip(s2, s4[1:])]
        centre = [4.0 * a + 6.0 * b for a, b in zip(s2[1:], s4[2:])][:count]
        above = [jnp.where(top, 0.0, shift_up(a)) for a in s2[1 : count + 1]]
        below = [jnp.where(bottom, 0.0, shift_down(a)) for a in s2[1 : count + 1]]
        scale = [factor * step[first + n] for n in range(count)]
        for v in range(NV):
            p = [state[v, first + n] for n in range(-2, count + 2)]
            r = [a * b for a, b in zip(side, p[1:])]
            q = [a * b for a, b in zip(s4, p)]
            for n in range(count):
                here = p[n + 2]
                change = (
                    flux[n][v]
                    + centre[n] * here
                    - (r[n] + r[n + 2])
                    + (q[n] + q[n + 4])
                    - (above[n] * shift_up(here) + below[n] * shift_down(here))
                    + source[v, first + n]
                )
                result[v, first + n] = anchor[v, first + n] - scale[n] * change
        flux = flux[count:]


def interior(active_len, matrix, states, fields):
    anchor = states[0]
    for s in range(3):
        lead = 2 * (s + 1)
        groups = lax.div(jnp.maximum(active_len - 2 * lead, 0) + (GROUP - 1), GROUP)

        def step(g, _, s=s, lead=lead):
            first = DEEP + lead + g * GROUP
            advance(FACTORS[s], matrix[...], [(first, GROUP)], anchor, states[s], states[s + 1], fields)
            return 0

        lax.fori_loop(0, groups, step, 0)


def boundary(active_len, matrix, states, fields):
    anchor = states[0]
    for s in range(3):
        lead = 2 * (s + 1)
        runs = [(lead, DEEP), (active_len + DEEP - lead, DEEP)]
        advance(FACTORS[s], matrix[...], runs, anchor, states[s], states[s + 1], fields)


def span_index(perm):
    marks = lax.broadcasted_iota(jnp.int32, (J, K), 1).astype(jnp.bfloat16)
    one_hot = perm.astype(jnp.float32).astype(jnp.bfloat16)
    found = lax.dot_general(marks, one_hot, (((1,), (1,)), ((), ())), preferred_element_type=jnp.float32)
    return found.astype(jnp.int32)


def take_span(values, index):
    return jnp.take_along_axis(values, index, axis=1, mode="promise_in_bounds")


def sides(active_len, on, cross):
    odd = odd_place()
    return ((odd, on), (jnp.logical_not(odd), cross))


def first_interior_kernel(
    lengths, jac, perm, state_in, source_in, second_in, fourth_in, step_in,
    index, matrix, state, source, second, fourth, step, one, two, three,
    sem,
):
    body = pl.ds(DEEP, SLOTS)
    copies = [
        pltpu.make_async_copy(state_in.at[0], state.at[:, body], sem.at[0]),
        pltpu.make_async_copy(second_in.at[0], second.at[body], sem.at[1]),
        pltpu.make_async_copy(fourth_in.at[0], fourth.at[body], sem.at[2]),
        pltpu.make_async_copy(source_in.at[0], source.at[:, body], sem.at[3]),
        pltpu.make_async_copy(step_in.at[0], step.at[body], sem.at[4]),
    ]
    for copy in copies:
        copy.start()
    for side in range(2):
        index[side] = span_index(perm[0, side])
    matrix[...] = flux_matrix(jac)
    for copy in copies:
        copy.wait()
    interior(lengths[0], matrix, (state, one, two, three), (source, second, fourth, step))


def first_boundary_kernel(
    lengths, index, matrix, on_got, cross_got, state_in, source_in, second_in, fourth_in, step_in, one_in, two_in, three_in,
    state, source, second, fourth, step, one, two, three, on_send, cross_send,
):
    active_len = lengths[0]
    refs = {"state": state, "source": source, "second": second, "fourth": fourth, "step": step}
    for before, got in sides(active_len, on_got, cross_got):
        perm = jnp.where(before, index[0], index[1])
        for name, field, at, depth in message_spans():
            ref = refs[name] if field is None else refs[name].at[field]
            base = jnp.where(before, DEEP - depth, active_len + DEEP)
            for layer in range(depth):
                ref[base + layer] = take_span(got[at + layer], perm)
    boundary(active_len, matrix, (state, one, two, three), (source, second, fourth, step))
    for lead, out in sides(active_len, on_send, cross_send):
        base = jnp.where(lead, DEEP, active_len)
        for v in range(NV):
            for layer in range(DEEP):
                out[v * DEEP + layer] = three[v, base + layer]


def second_interior_kernel(
    lengths, matrix, state, source, second, fourth, step, wall_grad,
    one, two, three, wall_start, wall,
):
    active_len = lengths[0]
    interior(active_len, matrix, (state, one, two, three), (source, second, fourth, step))
    body = pl.ds(DEEP, SLOTS)
    start = jnp.zeros((SLOTS, K), jnp.float32)
    more = jnp.zeros((SLOTS, K), jnp.float32)
    for v in range(NV):
        start = start + state[v, body, 0, :] * wall_grad[0, v]
        more = more + three[v, body, 0, :] * wall_grad[0, v]
    slot = lax.broadcasted_iota(jnp.int32, (SLOTS, K), 0)
    wall_start[...] = start
    wall[...] = jnp.where((slot >= DEEP) & (slot < active_len - DEEP), start + more, 0.0)


def second_boundary_kernel(
    lengths, weight, index, matrix, on_got, cross_got, source, second, fourth, step, wall_grad, wall_mask, wall_start, wall_in,
    state_in, one_in, two_in, three_in,
    state, one, two, three, wall,
    rows,
):
    active_len = lengths[0]
    for before, got in sides(active_len, on_got, cross_got):
        perm = jnp.where(before, index[0], index[1])
        base = jnp.where(before, 0, active_len + DEEP)
        for v in range(NV):
            for layer in range(DEEP):
                state[v, base + layer] = take_span(got[v * DEEP + layer], perm)
    boundary(active_len, matrix, (state, one, two, three), (source, second, fourth, step))
    rows[...] = wall_in[...]
    for base in (0, active_len - DEEP):
        for layer in range(DEEP):
            slot = pl.ds(base + layer, 1)
            total = wall_start[slot]
            for v in range(NV):
                total = total + three[v, base + layer + DEEP, pl.ds(0, 1), :] * wall_grad[0, v, slot]
            rows[slot] = total
    wall[...] = rows[...] * weight[0] * wall_mask[...].astype(jnp.float32)


def f32(*shape):
    return jax.ShapeDtypeStruct(shape, jnp.float32)


def call(kernel, name, outs, ins, out_specs=None, scratch=(), aliases=None):
    return pl.pallas_call(
        kernel, name=name, out_shape=outs, in_specs=ins, out_specs=out_specs or [VMEM] * len(outs),
        scratch_shapes=list(scratch), input_output_aliases=aliases or {}, compiler_params=PARAMS,
    )


def sum_over_conditions(value, adjoint, z_size, y_size):
    def pairs(z_to, y_to):
        return [(z * y_size + y, z_to(z) % z_size * y_size + y_to(y) % y_size) for z in range(z_size) for y in range(y_size)]

    def same(n):
        return n

    def move(value, z_to, y_to):
        return lax.ppermute(value, "cond", pairs(z_to, y_to))

    def gather_sum(value, groups):
        copies = jnp.broadcast_to(value[None], (len(groups[0]),) + value.shape)
        return lax.all_to_all(copies, "cond", 0, 0, tiled=True, axis_index_groups=groups).sum(0)

    value = value + move(value, lambda z: z ^ 1, same) + move(value, lambda z: z ^ 2, same) + move(value, lambda z: z ^ 3, same)
    value, adjoint = lax.optimization_barrier((value, adjoint))
    value = value + move(value, same, lambda y: y ^ 1) + move(value, same, lambda y: y ^ 2) + move(value, same, lambda y: y ^ 3)
    value = value + move(value, lambda z: 7 - z, same)
    return adjoint, value


def body(blocks, z_size, y_size, adjoint_in, source, second_coef, fourth_coef, time_step, jacobians, cond_weight, wall_grad,
         wall_mask, face_perm, lengths):
    chip = [(b, b ^ 1) for b in range(blocks)]
    cross = [(b, (b + (1 if b % 2 else -1)) % blocks) for b in range(blocks)]

    def exchange(on_send, cross_send):
        cross_got = lax.ppermute(cross_send, "blk", cross)
        return lax.ppermute(on_send, "blk", chip), cross_got

    planes, plane = f32(NV, EXT, J, K), f32(EXT, J, K)
    inputs = [pltpu.with_memory_space_constraint(x, pltpu.HBM) for x in (adjoint_in, source, second_coef, fourth_coef, time_step)]
    on_send, cross_send = call(
        pack_kernel, "pack_rims", [f32(PLANES, J, K)] * 2, [SMEM] + [HBM] * 5, scratch=[pltpu.SemaphoreType.DMA((2,))],
    )(lengths, *inputs)
    on_got, cross_got = exchange(on_send, cross_send)
    index, matrix, *arrays = call(
        first_interior_kernel, "first_interior",
        [jax.ShapeDtypeStruct((2, J, K), jnp.int32), jax.ShapeDtypeStruct((2 * ROWS, 4 * ROWS), jnp.bfloat16), planes, planes,
         plane, plane, plane, planes, planes, planes],
        [SMEM, SMEM, VMEM] + [HBM] * 5, scratch=[pltpu.SemaphoreType.DMA((5,))],
    )(lengths, jacobians, face_perm, *inputs)
    _, source_x, second_x, fourth_x, step_x, _, _, three, on_send, cross_send = call(
        first_boundary_kernel, "first_boundary",
        [planes, planes, plane, plane, plane, planes, planes, planes] + [f32(NV * DEEP, J, K)] * 2,
        [SMEM] + [VMEM] * 12, aliases={5 + n: n for n in range(8)},
    )(lengths, index, matrix, on_got, cross_got, *arrays)
    fields = (source_x, second_x, fourth_x, step_x)
    on_got, cross_got = exchange(on_send, cross_send)
    four, five, six, wall_start, wall = call(
        second_interior_kernel, "second_interior", [planes] * 3 + [f32(SLOTS, K)] * 2, [SMEM] + [VMEM] * 7,
    )(lengths, matrix, three, *fields, wall_grad)
    _, _, _, six, wall = call(
        second_boundary_kernel, "second_boundary", [planes] * 4 + [f32(SLOTS, K)],
        [SMEM] * 2 + [VMEM] * 16, scratch=[pltpu.VMEM((SLOTS, K), jnp.float32)], aliases={14 + n: n for n in range(4)},
    )(lengths, cond_weight, index, matrix, on_got, cross_got, *fields, wall_grad, wall_mask, wall_start, wall, three, four, five, six)
    active = lax.iota(jnp.int32, SLOTS) < lengths[0]
    adjoint = jnp.where(active[None, None, :, None, None], six[None, :, DEEP : DEEP + SLOTS], 0.0)
    return sum_over_conditions(wall, adjoint, z_size, y_size)


def solution(mesh):
    y_size = 4
    return jax.shard_map(
        functools.partial(body, mesh.shape["blk"], mesh.shape["cond"] // y_size, y_size),
        mesh=mesh,
        in_specs=(
            P("cond", None, "blk", None, None),
            P("cond", None, "blk", None, None),
            P("cond", "blk", None, None),
            P("cond", "blk", None, None),
            P("cond", "blk", None, None),
            P("cond", None, None, None),
            P("cond"),
            P("cond", None, "blk", None),
            P("blk", None),
            P("blk", None, None, None),
            P("blk"),
        ),
        out_specs=(P("cond", None, "blk", None, None), P("blk", None)),
        check_vma=False,
    )
```

```python
import functools

import jax
import jax.numpy as jnp
from jax import lax
from jax.experimental import pallas as pl
from jax.experimental.pallas import tpu as pltpu
from jax.sharding import PartitionSpec as P

NV = 6
SLOTS = 32
J = 8
K = 128
DEEP = 6
NEAR = 4
EXT = SLOTS + 2 * DEEP
PLANES = NV * DEEP + 2 * DEEP + NV * NEAR + NEAR
FACTORS = (0.6, 0.6, 1.0)
GROUP = 8
ROWS = NV * J

VMEM = pl.BlockSpec(memory_space=pltpu.VMEM)
SMEM = pl.BlockSpec(memory_space=pltpu.SMEM)
HBM = pl.BlockSpec(memory_space=pl.ANY)
PARAMS = pltpu.CompilerParams(vmem_limit_bytes=32 * 1024 * 1024)


def odd_place():
    return lax.rem(lax.axis_index("blk"), 2) == 1


def message_spans():
    at = 0
    for name, fields, depth in (("state", NV, DEEP), ("second", 1, DEEP), ("fourth", 1, DEEP), ("source", NV, NEAR), ("step", 1, NEAR)):
        for field in range(fields):
            yield name, field if fields > 1 else None, at, depth
            at += depth


def pack_kernel(lengths, state, source, second, fourth, step, cross_send, on_send, sem):
    refs = {"state": state, "source": source, "second": second, "fourth": fourth, "step": step}
    odd = odd_place()

    def start_copies(out, out_sem, tail):
        for name, field, at, depth in message_spans():
            ref = refs[name].at[0] if field is None else refs[name].at[0, field]
            first = lengths[0] - depth if tail else 0
            pltpu.make_async_copy(ref.at[pl.ds(first, depth)], out.at[pl.ds(at, depth)], out_sem).start()

    @pl.when(odd)
    def _():
        start_copies(on_send, sem.at[0], False)

    @pl.when(jnp.logical_not(odd))
    def _():
        start_copies(cross_send, sem.at[1], False)

    @pl.when(odd)
    def _():
        start_copies(cross_send, sem.at[1], True)

    @pl.when(jnp.logical_not(odd))
    def _():
        start_copies(on_send, sem.at[0], True)

    pltpu.make_async_copy(on_send, on_send, sem.at[0]).wait()
    pltpu.make_async_copy(cross_send, cross_send, sem.at[1]).wait()


def edge_rows():
    row = lax.broadcasted_iota(jnp.int32, (J, K), 0)
    return row == J - 1, row == 0


def shift_up(values):
    return pltpu.roll(values, J - 1, 0)


def shift_down(values):
    return pltpu.roll(values, 1, 0)


def two_parts(values):
    high = values.astype(jnp.bfloat16)
    return high, (values - high.astype(jnp.float32)).astype(jnp.bfloat16)


def flux_matrix(jac):
    width = 4 * ROWS
    lane = lax.broadcasted_iota(jnp.int32, (J, width), 1)
    row = lax.broadcasted_iota(jnp.int32, (J, width), 0)
    lane = jnp.where(lane >= 2 * ROWS, lane - 2 * ROWS, lane)
    pair = lane // J
    j = lane % J
    pattern = jnp.where(pair < NV, (j == row).astype(jnp.float32), (j == row + 1).astype(jnp.float32) - (j == row - 1).astype(jnp.float32))
    blocks = []
    for v in range(NV):
        block = jnp.zeros((J, width), jnp.float32)
        for axis in range(2):
            for u in range(NV):
                block = jnp.where(pair == axis * NV + u, -0.5 * jac[0, axis, u, v], block)
        blocks.append(block * pattern)
    high, low = two_parts(jnp.concatenate(blocks, 0))
    return jnp.concatenate([high, low], 0)


def flux_terms(matrix, state, cells):
    columns = []
    for e in cells:
        along = (state[:, e + 1] - state[:, e - 1]).reshape(ROWS, K)
        here = state[:, e].reshape(ROWS, K)
        high, low = two_parts(jnp.concatenate([along, here], 0))
        columns.append(jnp.concatenate([high, low], 0))
    product = jnp.dot(matrix, jnp.concatenate(columns, 1), preferred_element_type=jnp.float32)
    product = product[:ROWS] + product[ROWS:]
    return [[product[v * J : (v + 1) * J, n * K : (n + 1) * K] for v in range(NV)] for n in range(len(cells))]


def advance(factor, matrix, runs, anchor, state, result, fields):
    source, second, fourth, step = fields
    top, bottom = edge_rows()
    flux = flux_terms(matrix, state, [first + n for first, count in runs for n in range(count)])
    for first, count in runs:
        s2 = [second[first + n] for n in range(-1, count + 1)]
        s4 = [fourth[first + n] for n in range(-2, count + 2)]
        side = [a + 4.0 * b for a, b in zip(s2, s4[1:])]
        centre = [4.0 * a + 6.0 * b for a, b in zip(s2[1:], s4[2:])][:count]
        above = [jnp.where(top, 0.0, shift_up(a)) for a in s2[1 : count + 1]]
        below = [jnp.where(bottom, 0.0, shift_down(a)) for a in s2[1 : count + 1]]
        scale = [factor * step[first + n] for n in range(count)]
        for v in range(NV):
            p = [state[v, first + n] for n in range(-2, count + 2)]
            r = [a * b for a, b in zip(side, p[1:])]
            q = [a * b for a, b in zip(s4, p)]
            for n in range(count):
                here = p[n + 2]
                change = (
                    flux[n][v]
                    + centre[n] * here
                    - (r[n] + r[n + 2])
                    + (q[n] + q[n + 4])
                    - (above[n] * shift_up(here) + below[n] * shift_down(here))
                    + source[v, first + n]
                )
                result[v, first + n] = anchor[v, first + n] - scale[n] * change
        flux = flux[count:]


def interior(active_len, matrix, states, fields):
    anchor = states[0]
    for s in range(3):
        lead = 2 * (s + 1)
        groups = lax.div(jnp.maximum(active_len - 2 * lead, 0) + (GROUP - 1), GROUP)

        def step(g, _, s=s, lead=lead):
            first = DEEP + lead + g * GROUP
            advance(FACTORS[s], matrix[...], [(first, GROUP)], anchor, states[s], states[s + 1], fields)
            return 0

        lax.fori_loop(0, groups, step, 0)


def boundary(active_len, matrix, states, fields):
    anchor = states[0]
    for s in range(3):
        lead = 2 * (s + 1)
        runs = [(lead, DEEP), (active_len + DEEP - lead, DEEP)]
        advance(FACTORS[s], matrix[...], runs, anchor, states[s], states[s + 1], fields)


def span_index(perm):
    marks = lax.broadcasted_iota(jnp.int32, (J, K), 1).astype(jnp.bfloat16)
    one_hot = perm.astype(jnp.float32).astype(jnp.bfloat16)
    found = lax.dot_general(marks, one_hot, (((1,), (1,)), ((), ())), preferred_element_type=jnp.float32)
    return found.astype(jnp.int32)


def take_span(values, index):
    return jnp.take_along_axis(values, index, axis=1, mode="promise_in_bounds")


def sides(active_len, on, cross):
    odd = odd_place()
    return ((odd, on), (jnp.logical_not(odd), cross))


def first_interior_kernel(
    lengths, jac, perm, state_in, source_in, second_in, fourth_in, step_in,
    index, matrix, state, source, second, fourth, step, one, two, three,
    sem,
):
    body = pl.ds(DEEP, SLOTS)
    copies = [
        pltpu.make_async_copy(state_in.at[0], state.at[:, body], sem.at[0]),
        pltpu.make_async_copy(second_in.at[0], second.at[body], sem.at[1]),
        pltpu.make_async_copy(fourth_in.at[0], fourth.at[body], sem.at[2]),
        pltpu.make_async_copy(source_in.at[0], source.at[:, body], sem.at[3]),
        pltpu.make_async_copy(step_in.at[0], step.at[body], sem.at[4]),
    ]
    for copy in copies:
        copy.start()
    for side in range(2):
        index[side] = span_index(perm[0, side])
    matrix[...] = flux_matrix(jac)
    for copy in copies:
        copy.wait()
    interior(lengths[0], matrix, (state, one, two, three), (source, second, fourth, step))


def first_boundary_kernel(
    lengths, index, matrix, cross_got, on_got, state_in, source_in, second_in, fourth_in, step_in, one_in, two_in, three_in,
    state, source, second, fourth, step, one, two, three, cross_send, on_send,
):
    active_len = lengths[0]
    refs = {"state": state, "source": source, "second": second, "fourth": fourth, "step": step}
    for before, got in sides(active_len, on_got, cross_got):
        perm = jnp.where(before, index[0], index[1])
        for name, field, at, depth in message_spans():
            ref = refs[name] if field is None else refs[name].at[field]
            base = jnp.where(before, DEEP - depth, active_len + DEEP)
            for layer in range(depth):
                ref[base + layer] = take_span(got[at + layer], perm)
    boundary(active_len, matrix, (state, one, two, three), (source, second, fourth, step))
    for lead, out in sides(active_len, on_send, cross_send):
        base = jnp.where(lead, DEEP, active_len)
        for v in range(NV):
            for layer in range(DEEP):
                out[v * DEEP + layer] = three[v, base + layer]


def second_interior_kernel(
    lengths, matrix, state, source, second, fourth, step, wall_grad,
    one, two, three, wall_start, wall,
):
    active_len = lengths[0]
    interior(active_len, matrix, (state, one, two, three), (source, second, fourth, step))
    body = pl.ds(DEEP, SLOTS)
    start = jnp.zeros((SLOTS, K), jnp.float32)
    more = jnp.zeros((SLOTS, K), jnp.float32)
    for v in range(NV):
        start = start + state[v, body, 0, :] * wall_grad[0, v]
        more = more + three[v, body, 0, :] * wall_grad[0, v]
    slot = lax.broadcasted_iota(jnp.int32, (SLOTS, K), 0)
    wall_start[...] = start
    wall[...] = jnp.where((slot >= DEEP) & (slot < active_len - DEEP), start + more, 0.0)


def second_boundary_kernel(
    lengths, weight, index, matrix, cross_got, on_got, source, second, fourth, step, wall_grad, wall_mask, wall_start, wall_in,
    state_in, one_in, two_in, three_in,
    state, one, two, three, wall,
    rows,
):
    active_len = lengths[0]
    for before, got in sides(active_len, on_got, cross_got):
        perm = jnp.where(before, index[0], index[1])
        base = jnp.where(before, 0, active_len + DEEP)
        for v in range(NV):
            for layer in range(DEEP):
                state[v, base + layer] = take_span(got[v * DEEP + layer], perm)
    boundary(active_len, matrix, (state, one, two, three), (source, second, fourth, step))
    rows[...] = wall_in[...]
    for base in (0, active_len - DEEP):
        for layer in range(DEEP):
            slot = pl.ds(base + layer, 1)
            total = wall_start[slot]
            for v in range(NV):
                total = total + three[v, base + layer + DEEP, pl.ds(0, 1), :] * wall_grad[0, v, slot]
            rows[slot] = total
    wall[...] = rows[...] * weight[0] * wall_mask[...].astype(jnp.float32)


def f32(*shape):
    return jax.ShapeDtypeStruct(shape, jnp.float32)


def call(kernel, name, outs, ins, out_specs=None, scratch=(), aliases=None):
    return pl.pallas_call(
        kernel, name=name, out_shape=outs, in_specs=ins, out_specs=out_specs or [VMEM] * len(outs),
        scratch_shapes=list(scratch), input_output_aliases=aliases or {}, compiler_params=PARAMS,
    )


def sum_over_conditions(value, adjoint, z_size, y_size):
    def pairs(z_to, y_to):
        return [(z * y_size + y, z_to(z) % z_size * y_size + y_to(y) % y_size) for z in range(z_size) for y in range(y_size)]

    def same(n):
        return n

    def move(value, z_to, y_to):
        return lax.ppermute(value, "cond", pairs(z_to, y_to))

    def gather_sum(value, groups):
        copies = jnp.broadcast_to(value[None], (len(groups[0]),) + value.shape)
        return lax.all_to_all(copies, "cond", 0, 0, tiled=True, axis_index_groups=groups).sum(0)

    value = value + move(value, lambda z: z ^ 3, same) + move(value, lambda z: z ^ 2, same) + move(value, lambda z: z ^ 1, same)
    value, adjoint = lax.optimization_barrier((value, adjoint))
    value = value + move(value, same, lambda y: y ^ 2) + move(value, same, lambda y: y ^ 3) + move(value, same, lambda y: y ^ 1)
    value = value + move(value, lambda z: 7 - z, same)
    return adjoint, value


def body(blocks, z_size, y_size, adjoint_in, source, second_coef, fourth_coef, time_step, jacobians, cond_weight, wall_grad,
         wall_mask, face_perm, lengths):
    chip = [(b, b ^ 1) for b in range(blocks)]
    cross = [(b, (b + (1 if b % 2 else -1)) % blocks) for b in range(blocks)]

    def exchange(on_send, cross_send):
        cross_got = lax.ppermute(cross_send, "blk", cross)
        return lax.ppermute(on_send, "blk", chip), cross_got

    planes, plane = f32(NV, EXT, J, K), f32(EXT, J, K)
    inputs = [pltpu.with_memory_space_constraint(x, pltpu.HBM) for x in (adjoint_in, source, second_coef, fourth_coef, time_step)]
    cross_send, on_send = call(
        pack_kernel, "pack_rims", [f32(PLANES, J, K)] * 2, [SMEM] + [HBM] * 5, scratch=[pltpu.SemaphoreType.DMA((2,))],
    )(lengths, *inputs)
    on_got, cross_got = exchange(on_send, cross_send)
    index, matrix, *arrays = call(
        first_interior_kernel, "first_interior",
        [jax.ShapeDtypeStruct((2, J, K), jnp.int32), jax.ShapeDtypeStruct((2 * ROWS, 4 * ROWS), jnp.bfloat16), planes, planes,
         plane, plane, plane, planes, planes, planes],
        [SMEM, SMEM, VMEM] + [HBM] * 5, scratch=[pltpu.SemaphoreType.DMA((5,))],
    )(lengths, jacobians, face_perm, *inputs)
    _, source_x, second_x, fourth_x, step_x, _, _, three, cross_send, on_send = call(
        first_boundary_kernel, "first_boundary",
        [planes, planes, plane, plane, plane, planes, planes, planes] + [f32(NV * DEEP, J, K)] * 2,
        [SMEM] + [VMEM] * 12, aliases={5 + n: n for n in range(8)},
    )(lengths, index, matrix, cross_got, on_got, *arrays)
    fields = (source_x, second_x, fourth_x, step_x)
    on_got, cross_got = exchange(on_send, cross_send)
    four, five, six, wall_start, wall = call(
        second_interior_kernel, "second_interior", [planes] * 3 + [f32(SLOTS, K)] * 2, [SMEM] + [VMEM] * 7,
    )(lengths, matrix, three, *fields, wall_grad)
    _, _, _, six, wall = call(
        second_boundary_kernel, "second_boundary", [planes] * 4 + [f32(SLOTS, K)],
        [SMEM] * 2 + [VMEM] * 16, scratch=[pltpu.VMEM((SLOTS, K), jnp.float32)], aliases={14 + n: n for n in range(4)},
    )(lengths, cond_weight, index, matrix, cross_got, on_got, *fields, wall_grad, wall_mask, wall_start, wall, three, four, five, six)
    active = lax.iota(jnp.int32, SLOTS) < lengths[0]
    adjoint = jnp.where(active[None, None, :, None, None], six[None, :, DEEP : DEEP + SLOTS], 0.0)
    return sum_over_conditions(wall, adjoint, z_size, y_size)


def solution(mesh):
    y_size = 4
    return jax.shard_map(
        functools.partial(body, mesh.shape["blk"], mesh.shape["cond"] // y_size, y_size),
        mesh=mesh,
        in_specs=(
            P("cond", None, "blk", None, None),
            P("cond", None, "blk", None, None),
            P("cond", "blk", None, None),
            P("cond", "blk", None, None),
            P("cond", "blk", None, None),
            P("cond", None, None, None),
            P("cond"),
            P("cond", None, "blk", None),
            P("blk", None),
            P("blk", None, None, None),
            P("blk"),
        ),
        out_specs=(P("cond", None, "blk", None, None), P("blk", None)),
        check_vma=False,
    )
```

```python
import functools

import jax
import jax.numpy as jnp
from jax import lax
from jax.experimental import pallas as pl
from jax.experimental.pallas import tpu as pltpu
from jax.sharding import PartitionSpec as P

NV = 6
SLOTS = 32
J = 8
K = 128
DEEP = 6
NEAR = 4
EXT = SLOTS + 2 * DEEP
PLANES = NV * DEEP + 2 * DEEP + NV * NEAR + NEAR
FACTORS = (0.6, 0.6, 1.0)
GROUPS = (14, 12, 10)
ROWS = NV * J

VMEM = pl.BlockSpec(memory_space=pltpu.VMEM)
SMEM = pl.BlockSpec(memory_space=pltpu.SMEM)
HBM = pl.BlockSpec(memory_space=pl.ANY)
PARAMS = pltpu.CompilerParams(vmem_limit_bytes=32 * 1024 * 1024)


def odd_place():
    return lax.rem(lax.axis_index("blk"), 2) == 1


def message_spans():
    at = 0
    for name, fields, depth in (("state", NV, DEEP), ("second", 1, DEEP), ("fourth", 1, DEEP), ("source", NV, NEAR), ("step", 1, NEAR)):
        for field in range(fields):
            yield name, field if fields > 1 else None, at, depth
            at += depth


def pack_kernel(lengths, state, source, second, fourth, step, cross_send, on_send, sem):
    refs = {"state": state, "source": source, "second": second, "fourth": fourth, "step": step}
    odd = odd_place()

    def start_copies(out, out_sem, tail):
        for name, field, at, depth in message_spans():
            ref = refs[name].at[0] if field is None else refs[name].at[0, field]
            first = lengths[0] - depth if tail else 0
            pltpu.make_async_copy(ref.at[pl.ds(first, depth)], out.at[pl.ds(at, depth)], out_sem).start()

    @pl.when(odd)
    def _():
        start_copies(on_send, sem.at[0], False)

    @pl.when(jnp.logical_not(odd))
    def _():
        start_copies(cross_send, sem.at[1], False)

    @pl.when(odd)
    def _():
        start_copies(cross_send, sem.at[1], True)

    @pl.when(jnp.logical_not(odd))
    def _():
        start_copies(on_send, sem.at[0], True)

    pltpu.make_async_copy(on_send, on_send, sem.at[0]).wait()
    pltpu.make_async_copy(cross_send, cross_send, sem.at[1]).wait()


def edge_rows():
    row = lax.broadcasted_iota(jnp.int32, (J, K), 0)
    return row == J - 1, row == 0


def shift_up(values):
    return pltpu.roll(values, J - 1, 0)


def shift_down(values):
    return pltpu.roll(values, 1, 0)


def two_parts(values):
    high = values.astype(jnp.bfloat16)
    return high, (values - high.astype(jnp.float32)).astype(jnp.bfloat16)


def flux_matrix(jac):
    width = 4 * ROWS
    lane = lax.broadcasted_iota(jnp.int32, (J, width), 1)
    row = lax.broadcasted_iota(jnp.int32, (J, width), 0)
    lane = jnp.where(lane >= 2 * ROWS, lane - 2 * ROWS, lane)
    pair = lane // J
    j = lane % J
    pattern = jnp.where(pair < NV, (j == row).astype(jnp.float32), (j == row + 1).astype(jnp.float32) - (j == row - 1).astype(jnp.float32))
    blocks = []
    for v in range(NV):
        block = jnp.zeros((J, width), jnp.float32)
        for axis in range(2):
            for u in range(NV):
                block = jnp.where(pair == axis * NV + u, -0.5 * jac[0, axis, u, v], block)
        blocks.append(block * pattern)
    high, low = two_parts(jnp.concatenate(blocks, 0))
    return jnp.concatenate([high, low], 0)


def flux_terms(matrix, state, cells):
    columns = []
    for e in cells:
        along = (state[:, e + 1] - state[:, e - 1]).reshape(ROWS, K)
        here = state[:, e].reshape(ROWS, K)
        high, low = two_parts(jnp.concatenate([along, here], 0))
        columns.append(jnp.concatenate([high, low], 0))
    product = jnp.dot(matrix, jnp.concatenate(columns, 1), preferred_element_type=jnp.float32)
    product = product[:ROWS] + product[ROWS:]
    return [[product[v * J : (v + 1) * J, n * K : (n + 1) * K] for v in range(NV)] for n in range(len(cells))]


def advance(factor, matrix, runs, anchor, state, result, fields):
    source, second, fourth, step = fields
    top, bottom = edge_rows()
    flux = flux_terms(matrix, state, [first + n for first, count in runs for n in range(count)])
    for first, count in runs:
        s2 = [second[first + n] for n in range(-1, count + 1)]
        s4 = [fourth[first + n] for n in range(-2, count + 2)]
        side = [a + 4.0 * b for a, b in zip(s2, s4[1:])]
        centre = [4.0 * a + 6.0 * b for a, b in zip(s2[1:], s4[2:])][:count]
        above = [jnp.where(top, 0.0, shift_up(a)) for a in s2[1 : count + 1]]
        below = [jnp.where(bottom, 0.0, shift_down(a)) for a in s2[1 : count + 1]]
        scale = [factor * step[first + n] for n in range(count)]
        for v in range(NV):
            p = [state[v, first + n] for n in range(-2, count + 2)]
            r = [a * b for a, b in zip(side, p[1:])]
            q = [a * b for a, b in zip(s4, p)]
            for n in range(count):
                here = p[n + 2]
                change = (
                    flux[n][v]
                    + centre[n] * here
                    - (r[n] + r[n + 2])
                    + (q[n] + q[n + 4])
                    - (above[n] * shift_up(here) + below[n] * shift_down(here))
                    + source[v, first + n]
                )
                result[v, first + n] = anchor[v, first + n] - scale[n] * change
        flux = flux[count:]


def interior(active_len, matrix, states, fields):
    anchor = states[0]
    for s in range(3):
        lead = 2 * (s + 1)
        size = GROUPS[s]
        groups = lax.div(jnp.maximum(active_len - 2 * lead, 0) + (size - 1), size)

        def step(g, _, s=s, lead=lead, size=size):
            first = DEEP + lead + g * size
            advance(FACTORS[s], matrix[...], [(first, size)], anchor, states[s], states[s + 1], fields)
            return 0

        lax.fori_loop(0, groups, step, 0)


def boundary(active_len, matrix, states, fields):
    anchor = states[0]
    for s in range(3):
        lead = 2 * (s + 1)
        runs = [(lead, DEEP), (active_len + DEEP - lead, DEEP)]
        advance(FACTORS[s], matrix[...], runs, anchor, states[s], states[s + 1], fields)


def span_index(perm):
    marks = lax.broadcasted_iota(jnp.int32, (J, K), 1).astype(jnp.bfloat16)
    one_hot = perm.astype(jnp.float32).astype(jnp.bfloat16)
    found = lax.dot_general(marks, one_hot, (((1,), (1,)), ((), ())), preferred_element_type=jnp.float32)
    return found.astype(jnp.int32)


def take_span(values, index):
    return jnp.take_along_axis(values, index, axis=1, mode="promise_in_bounds")


def sides(active_len, on, cross):
    odd = odd_place()
    return ((odd, on), (jnp.logical_not(odd), cross))


def first_interior_kernel(
    lengths, jac, perm, state_in, source_in, second_in, fourth_in, step_in,
    index, matrix, state, source, second, fourth, step, one, two, three,
    sem,
):
    body = pl.ds(DEEP, SLOTS)
    copies = [
        pltpu.make_async_copy(state_in.at[0], state.at[:, body], sem.at[0]),
        pltpu.make_async_copy(second_in.at[0], second.at[body], sem.at[1]),
        pltpu.make_async_copy(fourth_in.at[0], fourth.at[body], sem.at[2]),
        pltpu.make_async_copy(source_in.at[0], source.at[:, body], sem.at[3]),
        pltpu.make_async_copy(step_in.at[0], step.at[body], sem.at[4]),
    ]
    for copy in copies:
        copy.start()
    for side in range(2):
        index[side] = span_index(perm[0, side])
    matrix[...] = flux_matrix(jac)
    for copy in copies:
        copy.wait()
    interior(lengths[0], matrix, (state, one, two, three), (source, second, fourth, step))


def first_boundary_kernel(
    lengths, index, matrix, cross_got, on_got, state_in, source_in, second_in, fourth_in, step_in, one_in, two_in, three_in,
    state, source, second, fourth, step, one, two, three, cross_send, on_send,
):
    active_len = lengths[0]
    refs = {"state": state, "source": source, "second": second, "fourth": fourth, "step": step}
    for before, got in sides(active_len, on_got, cross_got):
        perm = jnp.where(before, index[0], index[1])
        for name, field, at, depth in message_spans():
            ref = refs[name] if field is None else refs[name].at[field]
            base = jnp.where(before, DEEP - depth, active_len + DEEP)
            for layer in range(depth):
                ref[base + layer] = take_span(got[at + layer], perm)
    boundary(active_len, matrix, (state, one, two, three), (source, second, fourth, step))
    for lead, out in sides(active_len, on_send, cross_send):
        base = jnp.where(lead, DEEP, active_len)
        for v in range(NV):
            for layer in range(DEEP):
                out[v * DEEP + layer] = three[v, base + layer]


def second_interior_kernel(
    lengths, matrix, state, source, second, fourth, step, wall_grad,
    one, two, three, wall_start, wall,
):
    active_len = lengths[0]
    interior(active_len, matrix, (state, one, two, three), (source, second, fourth, step))
    body = pl.ds(DEEP, SLOTS)
    start = jnp.zeros((SLOTS, K), jnp.float32)
    more = jnp.zeros((SLOTS, K), jnp.float32)
    for v in range(NV):
        start = start + state[v, body, 0, :] * wall_grad[0, v]
        more = more + three[v, body, 0, :] * wall_grad[0, v]
    slot = lax.broadcasted_iota(jnp.int32, (SLOTS, K), 0)
    wall_start[...] = start
    wall[...] = jnp.where((slot >= DEEP) & (slot < active_len - DEEP), start + more, 0.0)


def second_boundary_kernel(
    lengths, weight, index, matrix, cross_got, on_got, source, second, fourth, step, wall_grad, wall_mask, wall_start, wall_in,
    state_in, one_in, two_in, three_in,
    state, one, two, three, wall,
    rows,
):
    active_len = lengths[0]
    for before, got in sides(active_len, on_got, cross_got):
        perm = jnp.where(before, index[0], index[1])
        base = jnp.where(before, 0, active_len + DEEP)
        for v in range(NV):
            for layer in range(DEEP):
                state[v, base + layer] = take_span(got[v * DEEP + layer], perm)
    boundary(active_len, matrix, (state, one, two, three), (source, second, fourth, step))
    rows[...] = wall_in[...]
    for base in (0, active_len - DEEP):
        for layer in range(DEEP):
            slot = pl.ds(base + layer, 1)
            total = wall_start[slot]
            for v in range(NV):
                total = total + three[v, base + layer + DEEP, pl.ds(0, 1), :] * wall_grad[0, v, slot]
            rows[slot] = total
    wall[...] = rows[...] * weight[0] * wall_mask[...].astype(jnp.float32)


def f32(*shape):
    return jax.ShapeDtypeStruct(shape, jnp.float32)


def call(kernel, name, outs, ins, out_specs=None, scratch=(), aliases=None):
    return pl.pallas_call(
        kernel, name=name, out_shape=outs, in_specs=ins, out_specs=out_specs or [VMEM] * len(outs),
        scratch_shapes=list(scratch), input_output_aliases=aliases or {}, compiler_params=PARAMS,
    )


def sum_over_conditions(value, adjoint, z_size, y_size):
    def pairs(z_to, y_to):
        return [(z * y_size + y, z_to(z) % z_size * y_size + y_to(y) % y_size) for z in range(z_size) for y in range(y_size)]

    def same(n):
        return n

    def move(value, z_to, y_to):
        return lax.ppermute(value, "cond", pairs(z_to, y_to))

    def gather_sum(value, groups):
        copies = jnp.broadcast_to(value[None], (len(groups[0]),) + value.shape)
        return lax.all_to_all(copies, "cond", 0, 0, tiled=True, axis_index_groups=groups).sum(0)

    value = value + move(value, lambda z: z ^ 2, same) + move(value, lambda z: z ^ 3, same) + move(value, lambda z: z ^ 1, same)
    value, adjoint = lax.optimization_barrier((value, adjoint))
    value = value + move(value, same, lambda y: y ^ 2) + move(value, same, lambda y: y ^ 1) + move(value, same, lambda y: y ^ 3)
    value = value + move(value, lambda z: 7 - z, same)
    return adjoint, value


def body(blocks, z_size, y_size, adjoint_in, source, second_coef, fourth_coef, time_step, jacobians, cond_weight, wall_grad,
         wall_mask, face_perm, lengths):
    chip = [(b, b ^ 1) for b in range(blocks)]
    cross = [(b, (b + (1 if b % 2 else -1)) % blocks) for b in range(blocks)]

    def exchange(on_send, cross_send):
        cross_got = lax.ppermute(cross_send, "blk", cross)
        return lax.ppermute(on_send, "blk", chip), cross_got

    planes, plane = f32(NV, EXT, J, K), f32(EXT, J, K)
    inputs = [pltpu.with_memory_space_constraint(x, pltpu.HBM) for x in (adjoint_in, source, second_coef, fourth_coef, time_step)]
    cross_send, on_send = call(
        pack_kernel, "pack_rims", [f32(PLANES, J, K)] * 2, [SMEM] + [HBM] * 5, scratch=[pltpu.SemaphoreType.DMA((2,))],
    )(lengths, *inputs)
    on_got, cross_got = exchange(on_send, cross_send)
    index, matrix, *arrays = call(
        first_interior_kernel, "first_interior",
        [jax.ShapeDtypeStruct((2, J, K), jnp.int32), jax.ShapeDtypeStruct((2 * ROWS, 4 * ROWS), jnp.bfloat16), planes, planes,
         plane, plane, plane, planes, planes, planes],
        [SMEM, SMEM, VMEM] + [HBM] * 5, scratch=[pltpu.SemaphoreType.DMA((5,))],
    )(lengths, jacobians, face_perm, *inputs)
    _, source_x, second_x, fourth_x, step_x, _, _, three, cross_send, on_send = call(
        first_boundary_kernel, "first_boundary",
        [planes, planes, plane, plane, plane, planes, planes, planes] + [f32(NV * DEEP, J, K)] * 2,
        [SMEM] + [VMEM] * 12, aliases={5 + n: n for n in range(8)},
    )(lengths, index, matrix, cross_got, on_got, *arrays)
    fields = (source_x, second_x, fourth_x, step_x)
    on_got, cross_got = exchange(on_send, cross_send)
    four, five, six, wall_start, wall = call(
        second_interior_kernel, "second_interior", [planes] * 3 + [f32(SLOTS, K)] * 2, [SMEM] + [VMEM] * 7,
    )(lengths, matrix, three, *fields, wall_grad)
    _, _, _, six, wall = call(
        second_boundary_kernel, "second_boundary", [planes] * 4 + [f32(SLOTS, K)],
        [SMEM] * 2 + [VMEM] * 16, scratch=[pltpu.VMEM((SLOTS, K), jnp.float32)], aliases={14 + n: n for n in range(4)},
    )(lengths, cond_weight, index, matrix, cross_got, on_got, *fields, wall_grad, wall_mask, wall_start, wall, three, four, five, six)
    active = lax.iota(jnp.int32, SLOTS) < lengths[0]
    adjoint = jnp.where(active[None, None, :, None, None], six[None, :, DEEP : DEEP + SLOTS], 0.0)
    return sum_over_conditions(wall, adjoint, z_size, y_size)


def solution(mesh):
    y_size = 4
    return jax.shard_map(
        functools.partial(body, mesh.shape["blk"], mesh.shape["cond"] // y_size, y_size),
        mesh=mesh,
        in_specs=(
            P("cond", None, "blk", None, None),
            P("cond", None, "blk", None, None),
            P("cond", "blk", None, None),
            P("cond", "blk", None, None),
            P("cond", "blk", None, None),
            P("cond", None, None, None),
            P("cond"),
            P("cond", None, "blk", None),
            P("blk", None),
            P("blk", None, None, None),
            P("blk"),
        ),
        out_specs=(P("cond", None, "blk", None, None), P("blk", None)),
        check_vma=False,
    )
```

```python
import functools

import jax
import jax.numpy as jnp
from jax import lax
from jax.experimental import pallas as pl
from jax.experimental.pallas import tpu as pltpu
from jax.sharding import PartitionSpec as P

NV = 6
SLOTS = 32
J = 8
K = 128
DEEP = 6
NEAR = 4
EXT = SLOTS + 2 * DEEP
PLANES = NV * DEEP + 2 * DEEP + NV * NEAR + NEAR
FACTORS = (0.6, 0.6, 1.0)
GROUPS = (14, 12, 10)
ROWS = NV * J

VMEM = pl.BlockSpec(memory_space=pltpu.VMEM)
SMEM = pl.BlockSpec(memory_space=pltpu.SMEM)
HBM = pl.BlockSpec(memory_space=pl.ANY)
PARAMS = pltpu.CompilerParams(vmem_limit_bytes=32 * 1024 * 1024)


def odd_place():
    return lax.rem(lax.axis_index("blk"), 2) == 1


def message_spans():
    at = 0
    for name, fields, depth in (("state", NV, DEEP), ("second", 1, DEEP), ("fourth", 1, DEEP), ("source", NV, NEAR), ("step", 1, NEAR)):
        for field in range(fields):
            yield name, field if fields > 1 else None, at, depth
            at += depth


def pack_kernel(lengths, state, source, second, fourth, step, cross_send, on_send, sem):
    refs = {"state": state, "source": source, "second": second, "fourth": fourth, "step": step}
    odd = odd_place()

    def start_copies(out, out_sem, tail):
        for name, field, at, depth in message_spans():
            ref = refs[name].at[0] if field is None else refs[name].at[0, field]
            first = lengths[0] - depth if tail else 0
            pltpu.make_async_copy(ref.at[pl.ds(first, depth)], out.at[pl.ds(at, depth)], out_sem).start()

    @pl.when(odd)
    def _():
        start_copies(on_send, sem.at[0], False)

    @pl.when(jnp.logical_not(odd))
    def _():
        start_copies(cross_send, sem.at[1], False)

    @pl.when(odd)
    def _():
        start_copies(cross_send, sem.at[1], True)

    @pl.when(jnp.logical_not(odd))
    def _():
        start_copies(on_send, sem.at[0], True)

    pltpu.make_async_copy(on_send, on_send, sem.at[0]).wait()
    pltpu.make_async_copy(cross_send, cross_send, sem.at[1]).wait()


def edge_rows():
    row = lax.broadcasted_iota(jnp.int32, (J, K), 0)
    return row == J - 1, row == 0


def shift_up(values):
    return pltpu.roll(values, J - 1, 0)


def shift_down(values):
    return pltpu.roll(values, 1, 0)


def two_parts(values):
    high = values.astype(jnp.bfloat16)
    return high, (values - high.astype(jnp.float32)).astype(jnp.bfloat16)


def flux_matrix(jac):
    width = 4 * ROWS
    lane = lax.broadcasted_iota(jnp.int32, (J, width), 1)
    row = lax.broadcasted_iota(jnp.int32, (J, width), 0)
    lane = jnp.where(lane >= 2 * ROWS, lane - 2 * ROWS, lane)
    pair = lane // J
    j = lane % J
    pattern = jnp.where(pair < NV, (j == row).astype(jnp.float32), (j == row + 1).astype(jnp.float32) - (j == row - 1).astype(jnp.float32))
    blocks = []
    for v in range(NV):
        block = jnp.zeros((J, width), jnp.float32)
        for axis in range(2):
            for u in range(NV):
                block = jnp.where(pair == axis * NV + u, -0.5 * jac[0, axis, u, v], block)
        blocks.append(block * pattern)
    high, low = two_parts(jnp.concatenate(blocks, 0))
    return jnp.concatenate([high, low], 0)


def flux_terms(matrix, state, cells):
    columns = []
    for e in cells:
        along = (state[:, e + 1] - state[:, e - 1]).reshape(ROWS, K)
        here = state[:, e].reshape(ROWS, K)
        high, low = two_parts(jnp.concatenate([along, here], 0))
        columns.append(jnp.concatenate([high, low], 0))
    product = jnp.dot(matrix, jnp.concatenate(columns, 1), preferred_element_type=jnp.float32)
    product = product[:ROWS] + product[ROWS:]
    return [[product[v * J : (v + 1) * J, n * K : (n + 1) * K] for v in range(NV)] for n in range(len(cells))]


def advance(factor, matrix, runs, anchor, state, result, fields):
    source, second, fourth, step = fields
    top, bottom = edge_rows()
    flux = flux_terms(matrix, state, [first + n for first, count in runs for n in range(count)])
    for first, count in runs:
        s2 = [second[first + n] for n in range(-1, count + 1)]
        s4 = [fourth[first + n] for n in range(-2, count + 2)]
        side = [a + 4.0 * b for a, b in zip(s2, s4[1:])]
        centre = [4.0 * a + 6.0 * b for a, b in zip(s2[1:], s4[2:])][:count]
        above = [jnp.where(top, 0.0, shift_up(a)) for a in s2[1 : count + 1]]
        below = [jnp.where(bottom, 0.0, shift_down(a)) for a in s2[1 : count + 1]]
        scale = [factor * step[first + n] for n in range(count)]
        for v in range(NV):
            p = [state[v, first + n] for n in range(-2, count + 2)]
            r = [a * b for a, b in zip(side, p[1:])]
            q = [a * b for a, b in zip(s4, p)]
            for n in range(count):
                here = p[n + 2]
                change = (
                    flux[n][v]
                    + centre[n] * here
                    - (r[n] + r[n + 2])
                    + (q[n] + q[n + 4])
                    - (above[n] * shift_up(here) + below[n] * shift_down(here))
                    + source[v, first + n]
                )
                result[v, first + n] = anchor[v, first + n] - scale[n] * change
        flux = flux[count:]


def interior(active_len, matrix, states, fields):
    anchor = states[0]
    for s in range(3):
        lead = 2 * (s + 1)
        size = GROUPS[s]
        groups = lax.div(jnp.maximum(active_len - 2 * lead, 0) + (size - 1), size)

        def step(g, _, s=s, lead=lead, size=size):
            first = DEEP + lead + g * size
            advance(FACTORS[s], matrix[...], [(first, size)], anchor, states[s], states[s + 1], fields)
            return 0

        lax.fori_loop(0, groups, step, 0)


def boundary(active_len, matrix, states, fields):
    anchor = states[0]
    for s in range(3):
        lead = 2 * (s + 1)
        runs = [(lead, DEEP), (active_len + DEEP - lead, DEEP)]
        advance(FACTORS[s], matrix[...], runs, anchor, states[s], states[s + 1], fields)


def span_index(perm):
    marks = lax.broadcasted_iota(jnp.int32, (J, K), 1).astype(jnp.bfloat16)
    one_hot = perm.astype(jnp.float32).astype(jnp.bfloat16)
    found = lax.dot_general(marks, one_hot, (((1,), (1,)), ((), ())), preferred_element_type=jnp.float32)
    return found.astype(jnp.int32)


def take_span(values, index):
    return jnp.take_along_axis(values, index, axis=1, mode="promise_in_bounds")


def sides(active_len, on, cross):
    odd = odd_place()
    return ((odd, on), (jnp.logical_not(odd), cross))


def first_interior_kernel(
    lengths, jac, perm, state_in, source_in, second_in, fourth_in, step_in,
    index, matrix, state, source, second, fourth, step, one, two, three,
    sem,
):
    body = pl.ds(DEEP, SLOTS)
    copies = [
        pltpu.make_async_copy(state_in.at[0], state.at[:, body], sem.at[0]),
        pltpu.make_async_copy(second_in.at[0], second.at[body], sem.at[1]),
        pltpu.make_async_copy(fourth_in.at[0], fourth.at[body], sem.at[2]),
        pltpu.make_async_copy(source_in.at[0], source.at[:, body], sem.at[3]),
        pltpu.make_async_copy(step_in.at[0], step.at[body], sem.at[4]),
    ]
    for copy in copies:
        copy.start()
    for side in range(2):
        index[side] = span_index(perm[0, side])
    matrix[...] = flux_matrix(jac)
    for copy in copies:
        copy.wait()
    interior(lengths[0], matrix, (state, one, two, three), (source, second, fourth, step))


def first_boundary_kernel(
    lengths, index, matrix, cross_got, on_got, state_in, source_in, second_in, fourth_in, step_in, one_in, two_in, three_in,
    state, source, second, fourth, step, one, two, three, cross_send, on_send,
):
    active_len = lengths[0]
    refs = {"state": state, "source": source, "second": second, "fourth": fourth, "step": step}
    for before, got in sides(active_len, on_got, cross_got):
        perm = jnp.where(before, index[0], index[1])
        for name, field, at, depth in message_spans():
            ref = refs[name] if field is None else refs[name].at[field]
            base = jnp.where(before, DEEP - depth, active_len + DEEP)
            for layer in range(depth):
                ref[base + layer] = take_span(got[at + layer], perm)
    boundary(active_len, matrix, (state, one, two, three), (source, second, fourth, step))
    for lead, out in sides(active_len, on_send, cross_send):
        base = jnp.where(lead, DEEP, active_len)
        for v in range(NV):
            for layer in range(DEEP):
                out[v * DEEP + layer] = three[v, base + layer]


def second_interior_kernel(
    lengths, matrix, state, source, second, fourth, step, wall_grad,
    one, two, three, wall_start, wall,
):
    active_len = lengths[0]
    interior(active_len, matrix, (state, one, two, three), (source, second, fourth, step))
    body = pl.ds(DEEP, SLOTS)
    start = jnp.zeros((SLOTS, K), jnp.float32)
    more = jnp.zeros((SLOTS, K), jnp.float32)
    for v in range(NV):
        start = start + state[v, body, 0, :] * wall_grad[0, v]
        more = more + three[v, body, 0, :] * wall_grad[0, v]
    slot = lax.broadcasted_iota(jnp.int32, (SLOTS, K), 0)
    wall_start[...] = start
    wall[...] = jnp.where((slot >= DEEP) & (slot < active_len - DEEP), start + more, 0.0)


def second_boundary_kernel(
    lengths, weight, index, matrix, cross_got, on_got, source, second, fourth, step, wall_grad, wall_mask, wall_start, wall_in,
    state_in, one_in, two_in, three_in,
    state, one, two, three, wall,
    rows,
):
    active_len = lengths[0]
    for before, got in sides(active_len, on_got, cross_got):
        perm = jnp.where(before, index[0], index[1])
        base = jnp.where(before, 0, active_len + DEEP)
        for v in range(NV):
            for layer in range(DEEP):
                state[v, base + layer] = take_span(got[v * DEEP + layer], perm)
    boundary(active_len, matrix, (state, one, two, three), (source, second, fourth, step))
    rows[...] = wall_in[...]
    for base in (0, active_len - DEEP):
        for layer in range(DEEP):
            slot = pl.ds(base + layer, 1)
            total = wall_start[slot]
            for v in range(NV):
                total = total + three[v, base + layer + DEEP, pl.ds(0, 1), :] * wall_grad[0, v, slot]
            rows[slot] = total
    wall[...] = rows[...] * weight[0] * wall_mask[...].astype(jnp.float32)


def f32(*shape):
    return jax.ShapeDtypeStruct(shape, jnp.float32)


def call(kernel, name, outs, ins, out_specs=None, scratch=(), aliases=None):
    return pl.pallas_call(
        kernel, name=name, out_shape=outs, in_specs=ins, out_specs=out_specs or [VMEM] * len(outs),
        scratch_shapes=list(scratch), input_output_aliases=aliases or {}, compiler_params=PARAMS,
    )


def sum_over_conditions(value, adjoint, z_size, y_size):
    def pairs(z_to, y_to):
        return [(z * y_size + y, z_to(z) % z_size * y_size + y_to(y) % y_size) for z in range(z_size) for y in range(y_size)]

    def same(n):
        return n

    def move(value, z_to, y_to):
        return lax.ppermute(value, "cond", pairs(z_to, y_to))

    def gather_sum(value, groups):
        copies = jnp.broadcast_to(value[None], (len(groups[0]),) + value.shape)
        return lax.all_to_all(copies, "cond", 0, 0, tiled=True, axis_index_groups=groups).sum(0)

    value = value + move(value, lambda z: z ^ 2, same) + move(value, lambda z: z ^ 3, same) + move(value, lambda z: z ^ 1, same)
    value, adjoint = lax.optimization_barrier((value, adjoint))
    value = value + move(value, same, lambda y: y ^ 2) + move(value, same, lambda y: y ^ 1) + move(value, same, lambda y: y ^ 3)
    far = {0: 7, 7: 0, 1: 4, 4: 1, 2: 5, 5: 2, 3: 6, 6: 3}
    value = value + move(value, lambda z: far[z], same)
    return adjoint, value


def body(blocks, z_size, y_size, adjoint_in, source, second_coef, fourth_coef, time_step, jacobians, cond_weight, wall_grad,
         wall_mask, face_perm, lengths):
    chip = [(b, b ^ 1) for b in range(blocks)]
    cross = [(b, (b + (1 if b % 2 else -1)) % blocks) for b in range(blocks)]

    def exchange(on_send, cross_send):
        cross_got = lax.ppermute(cross_send, "blk", cross)
        return lax.ppermute(on_send, "blk", chip), cross_got

    planes, plane = f32(NV, EXT, J, K), f32(EXT, J, K)
    inputs = [pltpu.with_memory_space_constraint(x, pltpu.HBM) for x in (adjoint_in, source, second_coef, fourth_coef, time_step)]
    cross_send, on_send = call(
        pack_kernel, "pack_rims", [f32(PLANES, J, K)] * 2, [SMEM] + [HBM] * 5, scratch=[pltpu.SemaphoreType.DMA((2,))],
    )(lengths, *inputs)
    on_got, cross_got = exchange(on_send, cross_send)
    index, matrix, *arrays = call(
        first_interior_kernel, "first_interior",
        [jax.ShapeDtypeStruct((2, J, K), jnp.int32), jax.ShapeDtypeStruct((2 * ROWS, 4 * ROWS), jnp.bfloat16), planes, planes,
         plane, plane, plane, planes, planes, planes],
        [SMEM, SMEM, VMEM] + [HBM] * 5, scratch=[pltpu.SemaphoreType.DMA((5,))],
    )(lengths, jacobians, face_perm, *inputs)
    _, source_x, second_x, fourth_x, step_x, _, _, three, cross_send, on_send = call(
        first_boundary_kernel, "first_boundary",
        [planes, planes, plane, plane, plane, planes, planes, planes] + [f32(NV * DEEP, J, K)] * 2,
        [SMEM] + [VMEM] * 12, aliases={5 + n: n for n in range(8)},
    )(lengths, index, matrix, cross_got, on_got, *arrays)
    fields = (source_x, second_x, fourth_x, step_x)
    on_got, cross_got = exchange(on_send, cross_send)
    four, five, six, wall_start, wall = call(
        second_interior_kernel, "second_interior", [planes] * 3 + [f32(SLOTS, K)] * 2, [SMEM] + [VMEM] * 7,
    )(lengths, matrix, three, *fields, wall_grad)
    _, _, _, six, wall = call(
        second_boundary_kernel, "second_boundary", [planes] * 4 + [f32(SLOTS, K)],
        [SMEM] * 2 + [VMEM] * 16, scratch=[pltpu.VMEM((SLOTS, K), jnp.float32)], aliases={14 + n: n for n in range(4)},
    )(lengths, cond_weight, index, matrix, cross_got, on_got, *fields, wall_grad, wall_mask, wall_start, wall, three, four, five, six)
    active = lax.iota(jnp.int32, SLOTS) < lengths[0]
    adjoint = jnp.where(active[None, None, :, None, None], six[None, :, DEEP : DEEP + SLOTS], 0.0)
    return sum_over_conditions(wall, adjoint, z_size, y_size)


def solution(mesh):
    y_size = 4
    return jax.shard_map(
        functools.partial(body, mesh.shape["blk"], mesh.shape["cond"] // y_size, y_size),
        mesh=mesh,
        in_specs=(
            P("cond", None, "blk", None, None),
            P("cond", None, "blk", None, None),
            P("cond", "blk", None, None),
            P("cond", "blk", None, None),
            P("cond", "blk", None, None),
            P("cond", None, None, None),
            P("cond"),
            P("cond", None, "blk", None),
            P("blk", None),
            P("blk", None, None, None),
            P("blk"),
        ),
        out_specs=(P("cond", None, "blk", None, None), P("blk", None)),
        check_vma=False,
    )
```
